128 devices in a mesh: blk: 16 (over x, y), aux: 8 (over z, core).
Axes of the slice: x: 4, y: 4, z: 4, core: 2. Of those that a mesh axis runs over, the one named last changes fastest.
Arguments:
- factors: float32 [80, 256, 32, 256], P('blk', 'aux'), may hold values from -6 to 6
- partners: int32 [64, 10], replicated, may hold values from -1 to 63, as said below
- block_owner: int32 [64], replicated, may hold values from 0 to 15, as said below
Outputs:
- pair_blocks: float32 [80, 10, 256, 256], P('blk', None, 'aux')
- diag_blocks: float32 [80, 256, 256], P('blk', 'aux')
The draws below stay inside these ranges and needn't reach their ends.
Inputs may be any that keep to these rules, and one draw needn't show every extreme that they name: `partners`: row a lists in increasing order the blocks c != a with |a - c| <= 5 that are significant with a, then -1 in the remaining slots; c is listed in row a exactly when a is listed in row c; some row lists 10 blocks. `block_owner`: never falls along the blocks; every index of blk holds 3 to 5 consecutive blocks, and some index holds exactly 5.
All inputs are finite; a program needn't handle non-finite values.
Results may differ from the reference program's by a relative error of at most 0.0003.
Values sent between devices are 32-bit elements; how exact they have to be, the bound alone decides.
A program may use at most 192 MiB of HBM per device.

```python
import math
import jax
import jax.numpy as jnp
from jax import lax

NB = 256
NOCC = 32
RMAX = 5
BLK_DEV = 4
SLOTS = 5
NBLK = 64
STORED = 80
NAUX = 256
N_BLK = 16


def draw_partners(key, part):
    key = jax.random.fold_in(key, 11)
    first_key, second_key = jax.random.split(key)
    radius = jax.random.randint(first_key, (NBLK,), 1, RMAX + 1)
    center = jax.random.randint(second_key, (), RMAX, NBLK - RMAX)
    block_ids = jnp.arange(NBLK, dtype=jnp.int32)
    radius = jnp.where(block_ids == center, RMAX, radius)
    offsets = jnp.concatenate([jnp.arange(-RMAX, 0, dtype=jnp.int32), jnp.arange(1, RMAX + 1, dtype=jnp.int32)])
    candidates = block_ids[:, None] + offsets[None, :]
    inside = (candidates >= 0) & (candidates < NBLK)
    clipped = jnp.clip(candidates, 0, NBLK - 1)
    widest = jnp.maximum(radius[:, None], radius[clipped])
    valid = inside & (jnp.abs(offsets)[None, :] <= widest)
    sorted_order = jnp.argsort(jnp.where(valid, 0, 1), axis=1, stable=True)
    packed = jnp.take_along_axis(candidates, sorted_order, axis=1)
    packed_valid = jnp.take_along_axis(valid, sorted_order, axis=1)
    return jnp.where(packed_valid, packed, -1).astype(jnp.int32)


def draw_block_owner(key, part):
    key = jax.random.fold_in(key, 23)
    first_key, second_key = jax.random.split(key)
    device_total = NBLK // BLK_DEV
    shuffled = jax.random.permutation(first_key, device_total)
    moves = jax.random.randint(second_key, (device_total // 2,), -1, 2)
    moves = moves.at[0].set(1)
    change = jnp.zeros((device_total,), jnp.int32)
    change = change.at[shuffled[0::2]].add(moves)
    change = change.at[shuffled[1::2]].add(-moves)
    ends = jnp.cumsum(BLK_DEV + change)
    block_ids = jnp.arange(NBLK, dtype=jnp.int32)
    return jnp.sum((ends[None, :] <= block_ids[:, None]).astype(jnp.int32), axis=1).astype(jnp.int32)


def with_spikes(entries, own_key, source, target, blocks, factor):
    def block_of(dim):
        return (jnp.arange(entries.shape[dim]) // (entries.shape[dim] // blocks)).reshape((-1,) + (1,) * (entries.ndim - 1 - dim))

    one_side = jax.random.permutation(own_key, blocks)[block_of(target)]
    far = (block_of(target) + blocks // 2) % blocks
    return jnp.where((block_of(source) == one_side) | (block_of(source) == far), factor * entries, entries)


def level_of(stream_key, extent, cuts, least, high):
    gain = 1.0
    for dim, blocks in cuts:
        draws = jax.random.uniform(jax.random.fold_in(jax.random.fold_in(stream_key, 6), dim), (blocks,), jnp.float32, least / len(cuts), high / len(cuts))
        gain = gain * jnp.repeat(jnp.exp(draws), extent[dim] // blocks).reshape((-1,) + (1,) * (len(extent) - 1 - dim))
    return gain


def heavy_noise(rng, extent, spread, limit, cuts, heavy, kind=jnp.bfloat16):
    drawn = spread * jax.random.normal(rng, extent, jnp.float32)
    if cuts:
        drawn = drawn * level_of(rng, extent, cuts, -0.22, 0.18)
    return jnp.clip(with_spikes(drawn, jax.random.fold_in(rng, 3), *heavy), -limit, limit).astype(kind)


def setup_inputs(seed: int = 0) -> dict:
    keys = jax.random.split(jax.random.key(seed), 4)
    factors = heavy_noise(keys[0], (STORED, NAUX, NOCC, NB), 1.0, 6.0, ((0, 16), (1, 8)), (1, 3, 8, 2.0), jnp.float32)
    partners = draw_partners(jax.random.fold_in(keys[3], 71), 0)
    block_owner = draw_block_owner(jax.random.fold_in(keys[3], 71), 0)
    return dict(factors=factors, partners=partners, block_owner=block_owner)


def reference(factors, partners, block_owner):
    devices = jnp.arange(N_BLK, dtype=jnp.int32)
    owned = block_owner[None, :] == devices[:, None]
    counts = lax.optimization_barrier(jnp.sum(owned.astype(jnp.int32), axis=1))
    firsts = lax.optimization_barrier(jnp.sum((block_owner[None, :] < devices[:, None]).astype(jnp.int32), axis=1))
    block_first = lax.optimization_barrier(jnp.sum(jnp.where(owned, firsts[:, None], 0), axis=0)).astype(jnp.int32)
    block_ids = jnp.arange(NBLK, dtype=jnp.int32)
    stored_slot = (block_owner * SLOTS + block_ids - block_first).astype(jnp.int32)
    matrices = factors.reshape(STORED, NAUX * NOCC, NB)
    scale_factor = 1.0 / math.sqrt(NAUX * NOCC)

    def per_block(index):
        own_rows = matrices[stored_slot[index]]
        diag_block = jnp.dot(own_rows.T, own_rows, precision=lax.Precision.HIGHEST, preferred_element_type=jnp.float32)
        uppers = []
        for offset in range(RMAX):
            other = jnp.minimum(index + 1 + offset, NBLK - 1).astype(jnp.int32)
            other_rows = matrices[stored_slot[other]]
            uppers.append(jnp.dot(own_rows.T, other_rows, precision=lax.Precision.HIGHEST, preferred_element_type=jnp.float32))
        return (diag_block, jnp.stack(uppers))
    diag_all, upper_all = lax.map(per_block, block_ids)

    def per_slot(slot):
        device = (slot // SLOTS).astype(jnp.int32)
        position = (slot % SLOTS).astype(jnp.int32)
        live = position < counts[device]
        block = jnp.minimum(firsts[device] + position, NBLK - 1).astype(jnp.int32)
        listed = partners[block]
        clipped = jnp.clip(listed, 0, NBLK - 1).astype(jnp.int32)
        above = listed > block
        below = (listed >= 0) & (listed < block)
        up_pick = upper_all[block, jnp.clip(clipped - block - 1, 0, RMAX - 1).astype(jnp.int32)]
        down_pick = jnp.swapaxes(upper_all[clipped, jnp.clip(block - clipped - 1, 0, RMAX - 1).astype(jnp.int32)], 1, 2)
        pair = jnp.where(above[:, None, None], up_pick, jnp.where(below[:, None, None], down_pick, 0.0))
        pair = jnp.where(live, pair, 0.0) * scale_factor
        diag_block = jnp.where(live, diag_all[block], 0.0) * scale_factor
        return (pair, diag_block)
    pair_blocks, diag_blocks = lax.map(per_slot, jnp.arange(STORED, dtype=jnp.int32))
    return (pair_blocks, diag_blocks)
```

```python
import functools
import math

import jax
import jax.numpy as jnp
import numpy as np
from jax import lax
from jax.experimental import pallas as pl
from jax.experimental.pallas import tpu as pltpu
from jax.sharding import PartitionSpec as P

MESH = pl.DeviceIdType.MESH
F32, BF16, I32 = jnp.float32, jnp.bfloat16, jnp.int32

SLOTS = 5
REACH = 5
RANKS = 8
ZDIM = 4
SHARD = 32

A1, A2, B1, B2, A3, B3 = 5, 6, 7, 8, 9, 10
FRONT, BACK = 16, 32


def _plan():
    near = [(t, t + d) for d in (1, 2) for t in range(SLOTS - d)]
    far = [(t, t + d) for d in (3, 4) for t in range(SLOTS - d)] + [(t, t) for t in range(SLOTS)]
    first = [(A1, BACK + s) for s in range(4)] + [(B1, FRONT + t) for t in (1, 2, 3)]
    second = [(A1, BACK + 4), (A2, BACK + 2), (A2, BACK + 3), (B1, FRONT + 4)]
    second += [(B2, FRONT + t) for t in (1, 2, 3)]
    last = [(A3, BACK + 2), (B3, FRONT + 2)]
    return [near, far, first, second, last]


PLAN = _plan()
SIZES = [len(group) for group in PLAN]
OFFS = [sum(SIZES[:g]) for g in range(len(PLAN))]
TOTAL = sum(SIZES)
QUADS = [2, 1, 2, 2, 1]
QOFFS = [sum(QUADS[:g]) for g in range(len(PLAN))]
NQUAD = sum(QUADS)
AHEAD = [0, 0, 4, 3, 1]
BEHIND = [0, 0, 3, 4, 1]
RES_T = 36
RES_FA = RES_T + 4 * NQUAD
RES_FB = RES_FA + 12
ZERO = RES_FB + 12
NRES = ZERO + 1


def _tables():
    row, column, from_a, from_b = {}, {}, {}, {}
    for g, group in enumerate(PLAN):
        for i, key in enumerate(group):
            row[key] = OFFS[g] + i
            column[key] = RES_T + 4 * QOFFS[g] + i
            if g >= 2 and i < AHEAD[g]:
                from_a[key] = RES_FA + 4 * (g - 2) + i
            elif g >= 2:
                from_b[key] = RES_FB + 4 * (g - 2) + i - AHEAD[g]
    table = np.full((3, SLOTS, 2 * REACH + 1, 2), ZERO, np.int32)
    aheads, behinds = (A1, A2, A3), (B1, B2, B3)
    for n in (3, 4, 5):
        for t in range(n):
            for d in range(1, REACH + 1):
                p = t + d
                if p < n:
                    places = [row[(t, p)]]
                else:
                    k, s = p - n + 1, n - 1 - t
                    places = []
                    if k <= 3 and (aheads[k - 1], BACK + s) in column:
                        places.append(column[(aheads[k - 1], BACK + s)])
                    if s <= 2 and (behinds[s], FRONT + k - 1) in from_b:
                        places.append(from_b[(behinds[s], FRONT + k - 1)])
                assert len(places) == (2 if p >= n and (k, s) == (3, 2) else 1), (n, t, d)
                table[n - 3, t, REACH + d, : len(places)] = places
                q = t - d
                if q >= 0:
                    places = [column[(q, t)]]
                else:
                    k = -q
                    places = []
                    if k <= 3 and (behinds[k - 1], FRONT + t) in column:
                        places.append(column[(behinds[k - 1], FRONT + t)])
                    if t <= 2 and (aheads[t], BACK + k - 1) in from_a:
                        places.append(from_a[(aheads[t], BACK + k - 1)])
                assert len(places) == (2 if q < 0 and (k, t) == (3, 2) else 1), (n, t, -d)
                table[n - 3, t, REACH - d, : len(places)] = places
    return table.reshape(-1)


TABLE = _tables()
NTAB = TABLE.shape[0]
LEFT = np.array([key[0] for group in PLAN for key in group], np.int32)
RIGHT = np.array([key[1] for group in PLAN for key in group], np.int32)
CONSTS = np.concatenate([TABLE, LEFT, RIGHT])


def kernel(
    blk_count,
    owner_ref,
    partners_ref,
    consts_ref,
    fac_ref,
    pair_ref,
    diag_ref,
    own,
    staged,
    inbox,
    left_hi,
    left_lo,
    right_hi,
    right_lo,
    lhalf_hi,
    lhalf_lo,
    parts,
    from_core,
    out_across,
    out_up,
    out_down,
    relay_up,
    relay_down,
    sum_up,
    sum_down,
    rows_of,
    from_before,
    from_after,
    t_out,
    t_in,
    res,
    right_at,
    place_at,
    own_sem,
    y_send,
    y_recv,
    c_send,
    c_recv,
    z1_send,
    z1_recv,
    z2_send,
    z2_recv,
    t_send,
    t_recv,
    f_send,
    f_recv,
):
    depth = own.shape[1]
    half = depth // 2
    blocks = owner_ref.shape[0]
    partner_slots = partners_ref.shape[1]
    scale = 1.0 / math.sqrt(RANKS * depth)

    b, r = lax.axis_index("blk"), lax.axis_index("aux")
    z, c = r // 2, r % 2
    after, before = (b + 1) % blk_count, (b + blk_count - 1) % blk_count
    up, down, across = (z + 1) % ZDIM, (z + 3) % ZDIM, (z + 2) % ZDIM
    dev_after, dev_before = (after, r), (before, r)
    dev_core = (b, 2 * z + 1 - c)
    dev_up, dev_down = (b, 2 * up + c), (b, 2 * down + c)

    own_copies = [pltpu.make_async_copy(fac_ref.at[t], own.at[t], own_sem.at[t]) for t in range(SLOTS)]
    for t in (4, 3, 2, 1, 0):
        own_copies[t].start()

    barrier = pltpu.get_barrier_semaphore()
    peers = [(b, (r + k) % RANKS) for k in range(1, RANKS)] + [dev_after, dev_before]
    for peer in peers:
        pl.semaphore_signal(barrier, inc=1, device_id=peer, device_id_type=MESH)

    def tally(i, carry):
        count, first = carry
        holder = owner_ref[i]
        return count + (holder == b).astype(I32), first + (holder < b).astype(I32)

    count, first = lax.fori_loop(0, blocks, tally, (jnp.int32(0), jnp.int32(0)))
    count = jnp.clip(count, 3, SLOTS)

    pl.semaphore_wait(barrier, len(peers))

    def remote(src, dst, send, recv, device):
        return pltpu.make_async_remote_copy(
            src_ref=src, dst_ref=dst, send_sem=send, recv_sem=recv, device_id=device, device_id_type=MESH
        )

    sends_a = [
        remote(fac_ref.at[0], inbox[0], y_send.at[0], y_recv.at[0], dev_before),
        remote(fac_ref.at[1], inbox[1], y_send.at[1], y_recv.at[1], dev_before),
        remote(fac_ref.at[2, pl.ds(0, half)], inbox[2], y_send.at[2], y_recv.at[2], dev_before),
    ]
    sends_b = [
        remote(staged[k], inbox[3 + k], y_send.at[3 + k], y_recv.at[3 + k], dev_after) for k in range(3)
    ]
    sends_a[0].start()
    for t in (4, 3, 2, 1, 0):
        own_copies[t].wait()

    for k in range(3):
        start = half if k == 2 else 0

        def stage(i, _, k=k, start=start):
            rows = pl.ds(pl.multiple_of(i * 64, 64), 64)
            staged[k][rows, :] = own[count - 1 - k, pl.ds(pl.multiple_of(start + i * 64, 64), 64), :]
            return 0

        lax.fori_loop(0, (depth - start) // 64, stage, 0)
        sends_b[k].start()
        if k < 2:
            sends_a[k + 1].start()

    def right_of(e, _):
        code = consts_ref[NTAB + TOTAL + e]
        s, t = code - BACK, code - FRONT
        from_back = jnp.where(s < count, count - 1 - s, B1 + s - count)
        from_front = jnp.where(t < count, t, A1 + t - count)
        right = jnp.where(code >= BACK, from_back, jnp.where(code >= FRONT, from_front, code))
        right_at[e] = jnp.clip(right, 0, B2)
        return 0

    lax.fori_loop(0, TOTAL, right_of, 0)

    def place_of(i, _):
        t, j = i // partner_slots, i % partner_slots
        a = jnp.clip(first + t, 0, blocks - 1)
        partner = partners_ref[a, j]
        d = jnp.clip(partner - a, -REACH, REACH)
        ok = (partner >= 0) & (t < count)
        at = (((count - 3) * SLOTS + t) * (2 * REACH + 1) + d + REACH) * 2
        at = jnp.clip(at, 0, NTAB - 2)
        place_at[2 * i] = jnp.where(ok, consts_ref[at], ZERO)
        place_at[2 * i + 1] = jnp.where(ok, consts_ref[at + 1], ZERO)
        return 0

    lax.fori_loop(0, SLOTS * partner_slots, place_of, 0)
    res[ZERO] = jnp.zeros(res.shape[1:], F32)

    step = 128

    def split(x):
        hi = x.astype(BF16)
        return hi, (x - hi.astype(F32)).astype(BF16)

    def prepare(load, at):
        def body(i, _):
            rows = pl.ds(pl.multiple_of(i * step, step), step)
            x = load(rows)
            right_hi[at, rows, :], right_lo[at, rows, :] = split(x)
            left_hi[at, :, rows], left_lo[at, :, rows] = split(x.T)
            return 0

        lax.fori_loop(0, depth // step, body, 0)

    def prepare_half(k):
        def body(i, _):
            rows = pl.ds(pl.multiple_of(i * step, step), step)
            lhalf_hi[k, :, rows], lhalf_lo[k, :, rows] = split(inbox[2 + 3 * k][rows, :].T)
            return 0

        lax.fori_loop(0, half // step, body, 0)

    def times(lh, ll, rh, rl):
        total = jnp.dot(lh, rh, preferred_element_type=F32)
        total += jnp.dot(lh, rl, preferred_element_type=F32)
        return total + jnp.dot(ll, rh, preferred_element_type=F32)

    def store(total, g, i):
        for rank in range(RANKS):
            parts[g][rank % 2, rank // 2, i] = total[rank * SHARD : (rank + 1) * SHARD]

    def over(g, body):
        def run(i, _):
            body(i)
            return 0

        lax.fori_loop(0, SIZES[g], run, 0)

    def products(g):
        def body(i):
            left, right = jnp.clip(consts_ref[NTAB + OFFS[g] + i], 0, B2), right_at[OFFS[g] + i]
            store(times(left_hi[left], left_lo[left], right_hi[right], right_lo[right]), g, i)

        over(g, body)

    def products_half(g):
        for k in range(2):
            right, rows = right_at[OFFS[g] + k], pl.ds(k * half, half)
            store(times(lhalf_hi[k], lhalf_lo[k], right_hi[right, rows, :], right_lo[right, rows, :]), g, k)

    def core_copy(g):
        return remote(parts[g].at[1 - c], from_core[g], c_send.at[g], c_recv.at[g], dev_core)

    def relay_copies(g):
        upper, lower = out_across[g].at[:, pl.ds(0, 16)], out_across[g].at[:, pl.ds(16, 16)]
        return (
            remote(upper, relay_up[g], z1_send.at[g, 0], z1_recv.at[g, 0], dev_up),
            remote(lower, relay_down[g], z1_send.at[g, 1], z1_recv.at[g, 1], dev_down),
        )

    def sum_copies(g):
        return (
            remote(out_up[g], sum_up[g], z2_send.at[g, 0], z2_recv.at[g, 0], dev_up),
            remote(out_down[g], sum_down[g], z2_send.at[g, 1], z2_recv.at[g, 1], dev_down),
        )

    def add_core(g):
        core_copy(g).wait_recv()

        def add_across(i):
            out_across[g][i] = parts[g][c, across, i] + from_core[g][across, i]

        over(g, add_across)
        for copy in relay_copies(g):
            copy.start()

    def add_relay(g):
        for copy in relay_copies(g):
            copy.wait_recv()

        def add(i):
            total = parts[g][c, up, i] + from_core[g][up, i]
            out_up[g][i, :16, :] = total[:16] + relay_up[g][i]
            out_up[g][i, 16:, :] = total[16:]
            total = parts[g][c, down, i] + from_core[g][down, i]
            out_down[g][i, :16, :] = total[:16]
            out_down[g][i, 16:, :] = total[16:] + relay_down[g][i]

        over(g, add)
        for copy in sum_copies(g):
            copy.start()

    def forward_copies(g):
        if not AHEAD[g]:
            return ()
        ahead, behind = pl.ds(0, AHEAD[g]), pl.ds(AHEAD[g], BEHIND[g])
        return (
            remote(rows_of[g].at[ahead], from_before[g - 2], f_send.at[g, 0], f_recv.at[g, 0], dev_after),
            remote(rows_of[g].at[behind], from_after[g - 2], f_send.at[g, 1], f_recv.at[g, 1], dev_before),
        )

    def turn_copy(g, k):
        to = (r + k) % RANKS
        return remote(t_out[g].at[to], t_in[g].at[r], t_send.at[g, k], t_recv.at[g, k], (b, to))

    def turn_arrival(g, k):
        to, source = (r + k) % RANKS, (r + RANKS - k) % RANKS
        return remote(t_out[g].at[to], t_in[g].at[source], t_send.at[g, k], t_recv.at[g, k], (b, to))

    def finish(g):
        for copy in sum_copies(g):
            copy.wait_recv()

        def add(i):
            total = (parts[g][c, z, i] + from_core[g][z, i]) + (sum_up[g][i] + sum_down[g][i])
            res[OFFS[g] + i] = total
            rows_of[g][i] = total

        over(g, add)
        for copy in forward_copies(g):
            copy.start()

        for q in range(QUADS[g]):
            at = OFFS[g] + 4 * q
            turned = res[at : at + 4].reshape(4 * SHARD, RANKS * SHARD).T
            for rank in range(RANKS):
                t_out[g][rank, q] = turned[rank * SHARD : (rank + 1) * SHARD]

        def send(k, _):
            turn_copy(g, k).start()
            return 0

        lax.fori_loop(1, RANKS, send, 0)

    def collect(g):
        def arrive(k, _):
            turn_arrival(g, k).wait_recv()
            return 0

        lax.fori_loop(1, RANKS, arrive, 0)
        t_in[g][r] = t_out[g][r]
        for q in range(QUADS[g]):
            pieces = [t_in[g][rank, q] for rank in range(RANKS)]
            for i in range(4):
                lanes = slice(SHARD * i, SHARD * (i + 1))
                at = RES_T + 4 * (QOFFS[g] + q) + i
                res[at] = jnp.concatenate([piece[:, lanes] for piece in pieces], axis=1)

    def prepare_own(t, _):
        prepare(lambda rows: own[t, rows, :], t)
        return 0

    lax.fori_loop(0, SLOTS, prepare_own, 0)
    for g in (0, 1):
        products(g)
        core_copy(g).start()
    for g in (0, 1):
        add_core(g)
    for g in (0, 1):
        add_relay(g)
    for g in (0, 1):
        finish(g)

    def arrived(k):
        sends_a[k].wait_recv()
        sends_b[k].wait_recv()

    def prepare_in(k):
        prepare(lambda rows: inbox[k][rows, :], A1 + k)
        prepare(lambda rows: inbox[3 + k][rows, :], B1 + k)

    arrived(0)
    prepare_in(0)
    products(2)
    core_copy(2).start()
    for g in (0, 1):
        collect(g)
    add_core(2)
    add_relay(2)
    finish(2)

    arrived(1)
    prepare_in(1)
    products(3)
    core_copy(3).start()
    collect(2)
    add_core(3)

    arrived(2)
    for k in range(2):
        prepare_half(k)
    products_half(4)
    core_copy(4).start()
    add_relay(3)
    add_core(4)
    finish(3)
    add_relay(4)
    finish(4)
    collect(3)
    collect(4)
    for g in (2, 3, 4):
        for copy in forward_copies(g):
            copy.wait_recv()
        for i in range(AHEAD[g]):
            res[RES_FA + 4 * (g - 2) + i] = from_before[g - 2][i]
        for i in range(BEHIND[g]):
            res[RES_FB + 4 * (g - 2) + i] = from_after[g - 2][i]

    def place(i, _):
        block = res[place_at[2 * i]] + res[place_at[2 * i + 1]]
        pair_ref[i // partner_slots, i % partner_slots] = block * scale
        return 0

    lax.fori_loop(0, SLOTS * partner_slots, place, 0)

    def place_diag(t, _):
        at = jnp.where(t < count, OFFS[1] + 3 + t, ZERO)
        diag_ref[t] = res[at] * scale
        return 0

    lax.fori_loop(0, SLOTS, place_diag, 0)

    for copy in sends_a + sends_b:
        copy.wait_send()
    for g in range(len(PLAN)):
        for copy in (core_copy(g), *relay_copies(g), *sum_copies(g), *forward_copies(g)):
            copy.wait_send()

        def sent(k, _, g=g):
            turn_copy(g, k).wait_send()
            return 0

        lax.fori_loop(1, RANKS, sent, 0)


def local(blk_count, factors, partners, block_owner):
    slots, aux_dev, occ, nb = factors.shape
    depth = aux_dev * occ
    half = depth // 2
    groups = len(PLAN)
    dma = pltpu.SemaphoreType.DMA
    smem, vmem = pl.BlockSpec(memory_space=pltpu.SMEM), pl.BlockSpec(memory_space=pltpu.VMEM)

    def room(*shape):
        return pltpu.VMEM((*shape, nb), F32)

    def by_group(*lead, rows=SHARD, sizes=SIZES):
        return [room(*lead, size, rows) for size in sizes]

    return pl.pallas_call(
        functools.partial(kernel, blk_count),
        out_shape=[
            jax.ShapeDtypeStruct((slots, partners.shape[1], SHARD, nb), F32),
            jax.ShapeDtypeStruct((slots, SHARD, nb), F32),
        ],
        in_specs=[smem, smem, smem, pl.BlockSpec(memory_space=pl.ANY)],
        out_specs=[vmem, vmem],
        scratch_shapes=[
            room(slots, depth),
            [room(depth), room(depth), room(half)],
            [room(depth), room(depth), room(half)] * 2,
            pltpu.VMEM((9, nb, depth), BF16),
            pltpu.VMEM((9, nb, depth), BF16),
            pltpu.VMEM((9, depth, nb), BF16),
            pltpu.VMEM((9, depth, nb), BF16),
            pltpu.VMEM((2, nb, half), BF16),
            pltpu.VMEM((2, nb, half), BF16),
            by_group(2, ZDIM),
            by_group(ZDIM),
            by_group(),
            by_group(),
            by_group(),
            by_group(rows=SHARD // 2),
            by_group(rows=SHARD // 2),
            by_group(),
            by_group(),
            by_group(),
            by_group(sizes=AHEAD[2:]),
            by_group(sizes=BEHIND[2:]),
            [pltpu.VMEM((RANKS, quads, SHARD, 4 * SHARD), F32) for quads in QUADS],
            [pltpu.VMEM((RANKS, quads, SHARD, 4 * SHARD), F32) for quads in QUADS],
            room(NRES, SHARD),
            pltpu.SMEM((TOTAL,), I32),
            pltpu.SMEM((2 * slots * partners.shape[1],), I32),
            dma((SLOTS,)),
            dma((6,)),
            dma((6,)),
            dma((groups,)),
            dma((groups,)),
            dma((groups, 2)),
            dma((groups, 2)),
            dma((groups, 2)),
            dma((groups, 2)),
            dma((groups, RANKS)),
            dma((groups, RANKS)),
            dma((groups, 2)),
            dma((groups, 2)),
        ],
        compiler_params=pltpu.CompilerParams(
            collective_id=0, has_side_effects=True, vmem_limit_bytes=60 * 1024 * 1024
        ),
    )(block_owner, partners, jnp.asarray(CONSTS), factors.reshape(slots, depth, nb))


def solution(mesh):
    in_specs = (P("blk", "aux", None, None), P(), P())
    out_specs = (P("blk", None, "aux", None), P("blk", "aux", None))
    return jax.shard_map(
        functools.partial(local, mesh.shape["blk"]),
        mesh=mesh,
        in_specs=in_specs,
        out_specs=out_specs,
        check_vma=False,
    )
```

```python
import functools
import math

import jax
import jax.numpy as jnp
import numpy as np
from jax import lax
from jax.experimental import pallas as pl
from jax.experimental.pallas import tpu as pltpu
from jax.sharding import PartitionSpec as P

MESH = pl.DeviceIdType.MESH
F32, BF16, I32 = jnp.float32, jnp.bfloat16, jnp.int32

SLOTS = 5
REACH = 5
RANKS = 8
ZDIM = 4
SHARD = 32

A1, A2, B1, B2, A3, B3 = 5, 6, 7, 8, 9, 10
FRONT, BACK = 16, 32


def _plan():
    own = [[(t, t + 1) for t in range(4)] + [(0, 0)]]
    own += [[(t, t + 2) for t in range(3)] + [(1, 1), (2, 2)]]
    own += [[(0, 3), (1, 4), (0, 4), (3, 3), (4, 4)]]
    first = [[(A1, BACK + s) for s in range(4)], [(B1, FRONT + t) for t in (1, 2, 3)]]
    second = [[(A2, BACK + 2), (A2, BACK + 3), (B2, FRONT + 1), (B2, FRONT + 2)]]
    second += [[(A1, BACK + 4), (B2, FRONT + 3), (B1, FRONT + 4)]]
    last = [[(A3, BACK + 2), (B3, FRONT + 2)]]
    return own + first + second + last


def _starts(sizes):
    return [sum(sizes[:g]) for g in range(len(sizes))]


PLAN = _plan()
GROUPS = len(PLAN)
LAST = GROUPS - 1
SIZES = [len(group) for group in PLAN]
OFFS = _starts(SIZES)
TOTAL = sum(SIZES)
AHEAD = [sum(key[0] in (A1, A2, A3) for key in group) for group in PLAN]
BEHIND = [sum(key[0] in (B1, B2, B3) for key in group) for group in PLAN]
RES_T = 36
RES_FA = [RES_T + 4 * GROUPS + start for start in _starts(AHEAD)]
RES_FB = [RES_FA[-1] + AHEAD[-1] + start for start in _starts(BEHIND)]
ZERO = RES_FB[-1] + BEHIND[-1]
NRES = ZERO + 1


def _tables():
    row, column, from_a, from_b = {}, {}, {}, {}
    for g, group in enumerate(PLAN):
        for i, key in enumerate(group):
            row[key] = OFFS[g] + i
            if i < 4:
                column[key] = RES_T + 4 * g + i
            if key[0] in (A1, A2, A3):
                from_a[key] = RES_FA[g] + i
            elif key[0] in (B1, B2, B3):
                from_b[key] = RES_FB[g] + i - AHEAD[g]
    table = np.full((3, SLOTS, 2 * REACH + 1, 2), ZERO, np.int32)
    aheads, behinds = (A1, A2, A3), (B1, B2, B3)
    for n in (3, 4, 5):
        for t in range(n):
            for d in range(1, REACH + 1):
                p = t + d
                if p < n:
                    places = [row[(t, p)]]
                else:
                    k, s = p - n + 1, n - 1 - t
                    places = []
                    if k <= 3 and (aheads[k - 1], BACK + s) in column:
                        places.append(column[(aheads[k - 1], BACK + s)])
                    if s <= 2 and (behinds[s], FRONT + k - 1) in from_b:
                        places.append(from_b[(behinds[s], FRONT + k - 1)])
                assert len(places) == (2 if p >= n and (k, s) == (3, 2) else 1), (n, t, d)
                table[n - 3, t, REACH + d, : len(places)] = places
                q = t - d
                if q >= 0:
                    places = [column[(q, t)]]
                else:
                    k = -q
                    places = []
                    if k <= 3 and (behinds[k - 1], FRONT + t) in column:
                        places.append(column[(behinds[k - 1], FRONT + t)])
                    if t <= 2 and (aheads[t], BACK + k - 1) in from_a:
                        places.append(from_a[(aheads[t], BACK + k - 1)])
                assert len(places) == (2 if q < 0 and (k, t) == (3, 2) else 1), (n, t, -d)
                table[n - 3, t, REACH - d, : len(places)] = places
    return np.concatenate([table.reshape(-1), [row[(t, t)] for t in range(SLOTS)]]).astype(np.int32)


TABLE = _tables()
NTAB = TABLE.shape[0]
DIAG = NTAB - SLOTS
LEFT = np.array([key[0] for group in PLAN for key in group], np.int32)
RIGHT = np.array([key[1] for group in PLAN for key in group], np.int32)
CONSTS = np.concatenate([TABLE, LEFT, RIGHT])


def kernel(
    blk_count,
    owner_ref,
    partners_hbm,
    consts_ref,
    fac_ref,
    pair_ref,
    diag_ref,
    partners_ref,
    head,
    own,
    staged,
    inbox,
    left_hi,
    left_lo,
    right_hi,
    right_lo,
    lhalf_hi,
    lhalf_lo,
    parts,
    from_core,
    out_across,
    out_up,
    out_down,
    relay_up,
    relay_down,
    sum_up,
    sum_down,
    rows_of,
    from_before,
    from_after,
    t_out,
    t_in,
    res,
    right_at,
    place_at,
    partners_sem,
    head_sem,
    own_sem,
    y_send,
    y_recv,
    c_send,
    c_recv,
    z1_send,
    z1_recv,
    z2_send,
    z2_recv,
    t_send,
    t_recv,
    f_send,
    f_recv,
):
    depth = own.shape[1]
    half = depth // 2
    blocks = owner_ref.shape[0]
    partner_slots = partners_ref.shape[0]
    scale = 1.0 / math.sqrt(RANKS * depth)

    b, r = lax.axis_index("blk"), lax.axis_index("aux")
    z, c = r // 2, r % 2
    after, before = (b + 1) % blk_count, (b + blk_count - 1) % blk_count
    up, down, across = (z + 1) % ZDIM, (z + 3) % ZDIM, (z + 2) % ZDIM
    dev_after, dev_before = (after, r), (before, r)
    dev_core = (b, 2 * z + 1 - c)
    dev_up, dev_down = (b, 2 * up + c), (b, 2 * down + c)

    head_copy = pltpu.make_async_copy(fac_ref.at[pl.ds(2, 3), pl.ds(0, half)], head, head_sem)
    head_copy.start()
    own_copies = [pltpu.make_async_copy(fac_ref.at[t], own.at[t], own_sem.at[t]) for t in range(SLOTS)]
    for t in (4, 3, 2, 1, 0):
        own_copies[t].start()

    partners_copy = pltpu.make_async_copy(partners_hbm, partners_ref, partners_sem)
    partners_copy.start()

    barrier = pltpu.get_barrier_semaphore()
    peers = [(b, (r + k) % RANKS) for k in range(1, RANKS)] + [dev_after, dev_before]
    for peer in peers:
        pl.semaphore_signal(barrier, inc=1, device_id=peer, device_id_type=MESH)

    def tally(i, carry):
        count, first = carry
        holder = owner_ref[i]
        return count + (holder == b).astype(I32), first + (holder < b).astype(I32)

    count, first = lax.fori_loop(0, blocks, tally, (jnp.int32(0), jnp.int32(0)))
    count = jnp.clip(count, 3, SLOTS)

    head_copy.wait()

    def stage_head(i, _):
        rows = pl.ds(pl.multiple_of(i * 64, 64), 64)
        staged[0][rows, :] = head[count - 3, rows, :]
        return 0

    lax.fori_loop(0, half // 64, stage_head, 0)
    pl.semaphore_wait(barrier, len(peers))

    def remote(src, dst, send, recv, device):
        return pltpu.make_async_remote_copy(
            src_ref=src, dst_ref=dst, send_sem=send, recv_sem=recv, device_id=device, device_id_type=MESH
        )

    chunks = [(k, half * i) for k, pieces in ((0, 2), (1, 2), (2, 1)) for i in range(pieces)]
    sends_a, sends_b = [], []
    for n, (k, start) in enumerate(chunks):
        rows = pl.ds(start, half)
        sends_a.append(remote(fac_ref.at[k, rows], inbox[k].at[rows], y_send.at[0, n], y_recv.at[0, n], dev_before))
        sends_b.append(
            remote(staged[k].at[rows], inbox[3 + k].at[rows], y_send.at[1, n], y_recv.at[1, n], dev_after)
        )

    sends_a[0].start()
    sends_b[0].start()
    for n in range(1, len(chunks)):
        sends_a[n].start()
    for t in (4, 3, 2, 1, 0):
        own_copies[t].wait()

    def stage(n):
        k, start = chunks[n]
        offset = half if k == 2 else 0

        def move(i, _):
            to = pl.ds(pl.multiple_of(start + i * 64, 64), 64)
            staged[k][to, :] = own[count - 1 - k, pl.ds(pl.multiple_of(start + offset + i * 64, 64), 64), :]
            return 0

        lax.fori_loop(0, half // 64, move, 0)

    for n in range(1, len(chunks)):
        stage(n)
        sends_b[n].start()

    def right_of(e, _):
        code = consts_ref[NTAB + TOTAL + e]
        s, t = code - BACK, code - FRONT
        from_back = jnp.where(s < count, count - 1 - s, B1 + s - count)
        from_front = jnp.where(t < count, t, A1 + t - count)
        right = jnp.where(code >= BACK, from_back, jnp.where(code >= FRONT, from_front, code))
        right_at[e] = jnp.clip(right, 0, B2)
        return 0


    def place_of(i, _):
        t, j = i // partner_slots, i % partner_slots
        a = jnp.clip(first + t, 0, blocks - 1)
        partner = partners_ref[j, a]
        d = jnp.clip(partner - a, -REACH, REACH)
        ok = (partner >= 0) & (t < count)
        at = (((count - 3) * SLOTS + t) * (2 * REACH + 1) + d + REACH) * 2
        at = jnp.clip(at, 0, DIAG - 2)
        place_at[2 * i] = jnp.where(ok, consts_ref[at], ZERO)
        place_at[2 * i + 1] = jnp.where(ok, consts_ref[at + 1], ZERO)
        return 0

    def look_up():
        lax.fori_loop(OFFS[3], TOTAL, right_of, 0)
        partners_copy.wait()
        lax.fori_loop(0, SLOTS * partner_slots, place_of, 0)
        res[ZERO] = jnp.zeros(res.shape[1:], F32)

    step = min(256, half)

    def split(x):
        hi = x.astype(BF16)
        return hi, (x - hi.astype(F32)).astype(BF16)

    def prepare(load, at, left=True, right=True):
        def body(i, _):
            rows = pl.ds(pl.multiple_of(i * step, step), step)
            x = load(rows)
            if right:
                right_hi[at, rows, :], right_lo[at, rows, :] = split(x)
            if left:
                left_hi[at, :, rows], left_lo[at, :, rows] = split(x.T)
            return 0

        lax.fori_loop(0, depth // step, body, 0)

    def prepare_half(k):
        def body(i, _):
            rows = pl.ds(pl.multiple_of(i * step, step), step)
            lhalf_hi[k, :, rows], lhalf_lo[k, :, rows] = split(inbox[2 + 3 * k][rows, :].T)
            return 0

        lax.fori_loop(0, half // step, body, 0)

    def times(lh, ll, rh, rl):
        total = jnp.dot(lh, rh, preferred_element_type=F32)
        total += jnp.dot(lh, rl, preferred_element_type=F32)
        return total + jnp.dot(ll, rh, preferred_element_type=F32)

    def store(total, g, i):
        for rank in range(RANKS):
            parts[g][rank % 2, rank // 2, i] = total[rank * SHARD : (rank + 1) * SHARD]

    def over(g, body):
        def run(i, _):
            body(i)
            return 0

        lax.fori_loop(0, SIZES[g], run, 0)

    def products(g):
        def body(i):
            left = jnp.clip(consts_ref[NTAB + OFFS[g] + i], 0, B2)
            right = jnp.clip(consts_ref[NTAB + TOTAL + i + OFFS[g]], 0, B2) if g < 3 else right_at[OFFS[g] + i]
            store(times(left_hi[left], left_lo[left], right_hi[right], right_lo[right]), g, i)

        over(g, body)

    def products_half(g):
        for k in range(2):
            right, rows = right_at[OFFS[g] + k], pl.ds(k * half, half)
            store(times(lhalf_hi[k], lhalf_lo[k], right_hi[right, rows, :], right_lo[right, rows, :]), g, k)

    def core_copy(g):
        return remote(parts[g].at[1 - c], from_core[g], c_send.at[g], c_recv.at[g], dev_core)

    def relay_copies(g):
        upper, lower = out_across[g].at[:, pl.ds(0, 16)], out_across[g].at[:, pl.ds(16, 16)]
        return (
            remote(upper, relay_up[g], z1_send.at[g, 0], z1_recv.at[g, 0], dev_up),
            remote(lower, relay_down[g], z1_send.at[g, 1], z1_recv.at[g, 1], dev_down),
        )

    def sum_copies(g):
        return (
            remote(out_up[g], sum_up[g], z2_send.at[g, 0], z2_recv.at[g, 0], dev_up),
            remote(out_down[g], sum_down[g], z2_send.at[g, 1], z2_recv.at[g, 1], dev_down),
        )

    def add_core(g):
        core_copy(g).wait_recv()

        def add_across(i):
            out_across[g][i] = parts[g][c, across, i] + from_core[g][across, i]

        over(g, add_across)
        for copy in relay_copies(g):
            copy.start()

    def add_relay(g):
        for copy in relay_copies(g):
            copy.wait_recv()

        def add(i):
            total = parts[g][c, up, i] + from_core[g][up, i]
            out_up[g][i, :16, :] = total[:16] + relay_up[g][i]
            out_up[g][i, 16:, :] = total[16:]
            total = parts[g][c, down, i] + from_core[g][down, i]
            out_down[g][i, :16, :] = total[:16]
            out_down[g][i, 16:, :] = total[16:] + relay_down[g][i]

        over(g, add)
        for copy in sum_copies(g):
            copy.start()

    def forward_copies(g):
        copies = []
        if AHEAD[g]:
            src = rows_of[g].at[pl.ds(0, AHEAD[g])]
            copies.append(remote(src, from_before[g], f_send.at[g, 0], f_recv.at[g, 0], dev_after))
        if BEHIND[g]:
            src = rows_of[g].at[pl.ds(AHEAD[g], BEHIND[g])]
            copies.append(remote(src, from_after[g], f_send.at[g, 1], f_recv.at[g, 1], dev_before))
        return copies

    def forward(g):
        for copy in forward_copies(g):
            copy.start()

    def turn_copy(g, k):
        to = (r + k) % RANKS
        return remote(t_out[g].at[to], t_in[g].at[r], t_send.at[g, k], t_recv.at[g, k], (b, to))

    def turn_arrival(g, k):
        to, source = (r + k) % RANKS, (r + RANKS - k) % RANKS
        return remote(t_out[g].at[to], t_in[g].at[source], t_send.at[g, k], t_recv.at[g, k], (b, to))

    def finish(g):
        for copy in sum_copies(g):
            copy.wait_recv()

        def add(i):
            total = (parts[g][c, z, i] + from_core[g][z, i]) + (sum_up[g][i] + sum_down[g][i])
            res[OFFS[g] + i] = total
            rows_of[g][i] = total

        over(g, add)
        if g == LAST:
            forward(g)
        turned = res[OFFS[g] : OFFS[g] + 4].reshape(4 * SHARD, RANKS * SHARD).T
        for rank in range(RANKS):
            t_out[g][rank] = turned[rank * SHARD : (rank + 1) * SHARD]

        def send(k, _):
            turn_copy(g, k).start()
            return 0

        lax.fori_loop(1, RANKS, send, 0)

    def collect(g):
        def arrive(k, _):
            turn_arrival(g, k).wait_recv()
            return 0

        lax.fori_loop(1, RANKS, arrive, 0)
        t_in[g][r] = t_out[g][r]
        pieces = [t_in[g][rank] for rank in range(RANKS)]
        for i in range(min(4, SIZES[g])):
            lanes = slice(SHARD * i, SHARD * (i + 1))
            res[RES_T + 4 * g + i] = jnp.concatenate([piece[:, lanes] for piece in pieces], axis=1)

    def prepare_own(t, _):
        prepare(lambda rows: own[t, rows, :], t)
        return 0

    def receive(g):
        for copy in forward_copies(g):
            copy.wait_recv()
        for i in range(AHEAD[g]):
            res[RES_FA[g] + i] = from_before[g][i]
        for i in range(BEHIND[g]):
            res[RES_FB[g] + i] = from_after[g][i]

    def place(start, stop):
        def body(i, _):
            block = res[place_at[2 * i]] + res[place_at[2 * i + 1]]
            pair_ref[i // partner_slots, i % partner_slots] = block * scale
            return 0

        lax.fori_loop(start * partner_slots, stop * partner_slots, body, 0)

    def place_diag():
        def body(t, _):
            at = jnp.where(t < count, jnp.clip(consts_ref[DIAG + t], 0, ZERO), ZERO)
            diag_ref[t] = res[at] * scale
            return 0

        lax.fori_loop(0, SLOTS, body, 0)

    lax.fori_loop(0, SLOTS, prepare_own, 0)

    def arrived(*numbers):
        for n in numbers:
            sends_a[n].wait_recv()
            sends_b[n].wait_recv()

    def prepare_in(k, **sides):
        prepare(lambda rows: inbox[k][rows, :], A1 + k, **sides)
        prepare(lambda rows: inbox[3 + k][rows, :], B1 + k, **sides)

    def multiply(g):
        products(g)
        core_copy(g).start()

    multiply(0)
    multiply(1)
    add_core(0)
    multiply(2)
    add_core(1)
    add_relay(0)
    add_core(2)
    add_relay(1)
    look_up()
    finish(0)
    add_relay(2)

    arrived(0, 1)
    prepare_in(0)
    multiply(3)
    finish(1)
    multiply(4)
    collect(0)
    add_core(3)
    finish(2)
    add_core(4)
    add_relay(3)
    collect(1)
    add_relay(4)
    collect(2)
    finish(3)
    finish(4)
    collect(3)
    collect(4)

    arrived(2, 3)
    prepare_in(1, right=False)
    multiply(5)
    prepare_in(1, left=False)
    multiply(6)
    add_core(5)
    add_core(6)
    add_relay(5)
    add_relay(6)

    arrived(4)
    for k in range(2):
        prepare_half(k)
    products_half(7)
    core_copy(7).start()
    for g in (3, 4):
        forward(g)
    finish(5)
    add_core(7)
    forward(5)
    finish(6)
    add_relay(7)
    forward(6)
    collect(5)
    finish(7)
    collect(6)
    for g in (3, 4, 5, 6):
        receive(g)
    place(3, SLOTS)
    place_diag()
    collect(7)
    receive(7)
    place(0, 3)

    for n in range(5):
        sends_a[n].wait_send()
        sends_b[n].wait_send()
    for g in range(len(PLAN)):
        for copy in (core_copy(g), *relay_copies(g), *sum_copies(g), *forward_copies(g)):
            copy.wait_send()

        def sent(k, _, g=g):
            turn_copy(g, k).wait_send()
            return 0

        lax.fori_loop(1, RANKS, sent, 0)


def local(blk_count, factors, partners, block_owner):
    slots, aux_dev, occ, nb = factors.shape
    depth = aux_dev * occ
    half = depth // 2
    groups = GROUPS
    dma = pltpu.SemaphoreType.DMA
    smem, vmem, hbm = (pl.BlockSpec(memory_space=space) for space in (pltpu.SMEM, pltpu.VMEM, pl.ANY))

    def room(*shape):
        return pltpu.VMEM((*shape, nb), F32)

    def by_group(*lead, rows=SHARD, sizes=SIZES):
        return [room(*lead, size, rows) for size in sizes]

    return pl.pallas_call(
        functools.partial(kernel, blk_count),
        out_shape=[
            jax.ShapeDtypeStruct((slots, partners.shape[1], SHARD, nb), F32),
            jax.ShapeDtypeStruct((slots, SHARD, nb), F32),
        ],
        in_specs=[smem, hbm, smem, hbm],
        out_specs=[vmem, vmem],
        scratch_shapes=[
            pltpu.SMEM(partners.shape[::-1], I32),
            room(3, half),
            room(slots, depth),
            [room(depth), room(depth), room(half)],
            [room(depth), room(depth), room(half)] * 2,
            pltpu.VMEM((9, nb, depth), BF16),
            pltpu.VMEM((9, nb, depth), BF16),
            pltpu.VMEM((9, depth, nb), BF16),
            pltpu.VMEM((9, depth, nb), BF16),
            pltpu.VMEM((2, nb, half), BF16),
            pltpu.VMEM((2, nb, half), BF16),
            by_group(2, ZDIM),
            by_group(ZDIM),
            by_group(),
            by_group(),
            by_group(),
            by_group(rows=SHARD // 2),
            by_group(rows=SHARD // 2),
            by_group(),
            by_group(),
            by_group(),
            by_group(sizes=[max(1, size) for size in AHEAD]),
            by_group(sizes=[max(1, size) for size in BEHIND]),
            [pltpu.VMEM((RANKS, SHARD, 4 * SHARD), F32)] * GROUPS,
            [pltpu.VMEM((RANKS, SHARD, 4 * SHARD), F32)] * GROUPS,
            room(NRES, SHARD),
            pltpu.SMEM((TOTAL,), I32),
            pltpu.SMEM((2 * slots * partners.shape[1],), I32),
            dma,
            dma,
            dma((SLOTS,)),
            dma((2, 5)),
            dma((2, 5)),
            dma((groups,)),
            dma((groups,)),
            dma((groups, 2)),
            dma((groups, 2)),
            dma((groups, 2)),
            dma((groups, 2)),
            dma((groups, RANKS)),
            dma((groups, RANKS)),
            dma((groups, 2)),
            dma((groups, 2)),
        ],
        compiler_params=pltpu.CompilerParams(
            collective_id=0, has_side_effects=True, vmem_limit_bytes=60 * 1024 * 1024
        ),
    )(block_owner, partners.T, jnp.asarray(CONSTS), factors.reshape(slots, depth, nb))


def solution(mesh):
    in_specs = (P("blk", "aux", None, None), P(), P())
    out_specs = (P("blk", None, "aux", None), P("blk", "aux", None))
    return jax.shard_map(
        functools.partial(local, mesh.shape["blk"]),
        mesh=mesh,
        in_specs=in_specs,
        out_specs=out_specs,
        check_vma=False,
    )
```

```python
import functools
import math

import jax
import jax.numpy as jnp
import numpy as np
from jax import lax
from jax.experimental import pallas as pl
from jax.experimental.pallas import tpu as pltpu
from jax.sharding import PartitionSpec as P

MESH = pl.DeviceIdType.MESH
F32, BF16, I32 = jnp.float32, jnp.bfloat16, jnp.int32

SLOTS = 5
REACH = 5
RANKS = 8
ZDIM = 4
SHARD = 32

A1, A2, B1, B2, A3, B3 = 5, 6, 7, 8, 9, 10
FRONT, BACK = 16, 32


def _plan():
    own = [[(t, t + 1) for t in range(4)] + [(0, 0)]]
    own += [[(t, t + 2) for t in range(3)] + [(1, 1), (2, 2)]]
    own += [[(0, 3), (1, 4), (0, 4), (3, 3), (4, 4)]]
    first = [[(A1, BACK + s) for s in range(4)], [(B1, FRONT + t) for t in (1, 2, 3)]]
    second = [[(A2, BACK + 2), (A2, BACK + 3), (B2, FRONT + 1), (B2, FRONT + 2)]]
    second += [[(A1, BACK + 4), (B2, FRONT + 3), (B1, FRONT + 4)]]
    last = [[(A3, BACK + 2), (B3, FRONT + 2)]]
    return own + first + second + last


def _starts(sizes):
    return [sum(sizes[:g]) for g in range(len(sizes))]


PLAN = _plan()
GROUPS = len(PLAN)
LAST = GROUPS - 1
SIZES = [len(group) for group in PLAN]
OFFS = _starts(SIZES)
TOTAL = sum(SIZES)
AHEAD = [sum(key[0] in (A1, A2, A3) for key in group) for group in PLAN]
BEHIND = [sum(key[0] in (B1, B2, B3) for key in group) for group in PLAN]
RES_T = 36
RES_FA = [RES_T + 4 * GROUPS + start for start in _starts(AHEAD)]
RES_FB = [RES_FA[-1] + AHEAD[-1] + start for start in _starts(BEHIND)]
ZERO = RES_FB[-1] + BEHIND[-1]
NRES = ZERO + 1


def _tables():
    row, column, from_a, from_b = {}, {}, {}, {}
    for g, group in enumerate(PLAN):
        for i, key in enumerate(group):
            row[key] = OFFS[g] + i
            if i < 4:
                column[key] = RES_T + 4 * g + i
            if key[0] in (A1, A2, A3):
                from_a[key] = RES_FA[g] + i
            elif key[0] in (B1, B2, B3):
                from_b[key] = RES_FB[g] + i - AHEAD[g]
    table = np.full((3, SLOTS, 2 * REACH + 1, 2), ZERO, np.int32)
    aheads, behinds = (A1, A2, A3), (B1, B2, B3)
    for n in (3, 4, 5):
        for t in range(n):
            for d in range(1, REACH + 1):
                p = t + d
                if p < n:
                    places = [row[(t, p)]]
                else:
                    k, s = p - n + 1, n - 1 - t
                    places = []
                    if k <= 3 and (aheads[k - 1], BACK + s) in column:
                        places.append(column[(aheads[k - 1], BACK + s)])
                    if s <= 2 and (behinds[s], FRONT + k - 1) in from_b:
                        places.append(from_b[(behinds[s], FRONT + k - 1)])
                assert len(places) == (2 if p >= n and (k, s) == (3, 2) else 1), (n, t, d)
                table[n - 3, t, REACH + d, : len(places)] = places
                q = t - d
                if q >= 0:
                    places = [column[(q, t)]]
                else:
                    k = -q
                    places = []
                    if k <= 3 and (behinds[k - 1], FRONT + t) in column:
                        places.append(column[(behinds[k - 1], FRONT + t)])
                    if t <= 2 and (aheads[t], BACK + k - 1) in from_a:
                        places.append(from_a[(aheads[t], BACK + k - 1)])
                assert len(places) == (2 if q < 0 and (k, t) == (3, 2) else 1), (n, t, -d)
                table[n - 3, t, REACH - d, : len(places)] = places
    return np.concatenate([table.reshape(-1), [row[(t, t)] for t in range(SLOTS)]]).astype(np.int32)


TABLE = _tables()
NTAB = TABLE.shape[0]
DIAG = NTAB - SLOTS
LEFT = np.array([key[0] for group in PLAN for key in group], np.int32)
RIGHT = np.array([key[1] for group in PLAN for key in group], np.int32)
CONSTS = np.concatenate([TABLE, LEFT, RIGHT])


def kernel(
    blk_count,
    owner_hbm,
    partners_hbm,
    consts_hbm,
    fac_ref,
    pair_hbm,
    diag_hbm,
    owner_ref,
    partners_ref,
    consts_ref,
    pair_ref,
    diag_ref,
    head,
    own,
    staged,
    inbox,
    left_hi,
    left_lo,
    right_hi,
    right_lo,
    lthird_hi,
    lthird_lo,
    parts,
    from_core,
    out_across,
    out_up,
    out_down,
    relay_up,
    relay_down,
    sum_up,
    sum_down,
    rows_of,
    from_before,
    from_after,
    third,
    third_rows,
    third_up,
    third_down,
    third_relay,
    third_sums,
    third_own,
    t_out,
    t_in,
    res,
    right_at,
    place_at,
    scalar_sem,
    out_sem,
    head_sem,
    own_sem,
    y_send,
    y_recv,
    c_send,
    c_recv,
    z1_send,
    z1_recv,
    z2_send,
    z2_recv,
    t_send,
    t_recv,
    f_send,
    f_recv,
    l_send,
    l_recv,
):
    depth = own.shape[1]
    half = depth // 2
    blocks = owner_ref.shape[0]
    partner_slots = partners_ref.shape[0]
    scale = 1.0 / math.sqrt(RANKS * depth)

    b, r = lax.axis_index("blk"), lax.axis_index("aux")
    z, c = r // 2, r % 2
    after, before = (b + 1) % blk_count, (b + blk_count - 1) % blk_count
    up, down, across = (z + 1) % ZDIM, (z + 3) % ZDIM, (z + 2) % ZDIM
    dev_after, dev_before = (after, r), (before, r)
    dev_core = (b, 2 * z + 1 - c)
    dev_up, dev_down = (b, 2 * up + c), (b, 2 * down + c)

    owner_copy = pltpu.make_async_copy(owner_hbm, owner_ref, scalar_sem.at[0])
    owner_copy.start()
    partners_copy = pltpu.make_async_copy(partners_hbm, partners_ref, scalar_sem.at[1])
    consts_copy = pltpu.make_async_copy(consts_hbm, consts_ref, scalar_sem.at[2])
    head_copy = pltpu.make_async_copy(fac_ref.at[pl.ds(2, 3), pl.ds(0, half)], head, head_sem)
    head_copy.start()
    own_copies = [pltpu.make_async_copy(fac_ref.at[t], own.at[t], own_sem.at[t]) for t in range(SLOTS)]
    for t in (4, 3, 2, 1, 0):
        own_copies[t].start()

    barrier = pltpu.get_barrier_semaphore()
    peers = [(b, (r + k) % RANKS) for k in range(1, RANKS)] + [dev_after, dev_before]
    for peer in peers:
        pl.semaphore_signal(barrier, inc=1, device_id=peer, device_id_type=MESH)

    partners_copy.start()
    consts_copy.start()
    owner_copy.wait()

    def tally(i, carry):
        count, first = carry
        holder = owner_ref[i]
        return count + (holder == b).astype(I32), first + (holder < b).astype(I32)

    count, first = lax.fori_loop(0, blocks, tally, (jnp.int32(0), jnp.int32(0)))
    count = jnp.clip(count, 3, SLOTS)

    head_copy.wait()

    def stage_head(i, _):
        rows = pl.ds(pl.multiple_of(i * 64, 64), 64)
        staged[0][rows, :] = head[count - 3, rows, :]
        return 0

    lax.fori_loop(0, half // 64, stage_head, 0)
    pl.semaphore_wait(barrier, len(peers))

    def remote(src, dst, send, recv, device):
        return pltpu.make_async_remote_copy(
            src_ref=src, dst_ref=dst, send_sem=send, recv_sem=recv, device_id=device, device_id_type=MESH
        )

    chunks = [(k, half * i) for k in range(2) for i in range(2)]
    sends_a, sends_b = [], []
    for n, (k, start) in enumerate(chunks):
        rows = pl.ds(start, half)
        sends_a.append(remote(fac_ref.at[k, rows], inbox[k].at[rows], y_send.at[0, n], y_recv.at[0, n], dev_before))
        sends_b.append(
            remote(staged[k].at[rows], inbox[2 + k].at[rows], y_send.at[1, n], y_recv.at[1, n], dev_after)
        )

    third_a, third_b = [], []
    for n in range(2):
        rows, sems = pl.ds(half * n, half), (y_send.at[0, 4 + n], y_recv.at[0, 4 + n])
        third_a.append(remote(fac_ref.at[2, rows], third.at[rows], *sems, dev_before))
        third_b.append(remote(staged[2].at[rows], third.at[rows], *sems, dev_after))

    sends_a[0].start()
    sends_b[0].start()
    for n in range(1, len(chunks)):
        sends_a[n].start()

    @pl.when(c == 0)
    def _():
        for copy in third_a:
            copy.start()

    for t in (4, 3, 2, 1, 0):
        own_copies[t].wait()

    def stage(k, start):
        def move(i, _):
            rows = pl.ds(pl.multiple_of(start + i * 64, 64), 64)
            staged[k][rows, :] = own[count - 1 - k, rows, :]
            return 0

        lax.fori_loop(0, half // 64, move, 0)

    for n in range(1, len(chunks)):
        stage(*chunks[n])
        sends_b[n].start()

    @pl.when(c == 1)
    def _():
        for n in range(2):
            stage(2, half * n)
            third_b[n].start()

    def right_of(e, _):
        code = consts_ref[NTAB + TOTAL + e]
        s, t = code - BACK, code - FRONT
        from_back = jnp.where(s < count, count - 1 - s, B1 + s - count)
        from_front = jnp.where(t < count, t, A1 + t - count)
        right = jnp.where(code >= BACK, from_back, jnp.where(code >= FRONT, from_front, code))
        right_at[e] = jnp.clip(right, 0, B2)
        return 0


    def place_of(i, _):
        t, j = i // partner_slots, i % partner_slots
        a = jnp.clip(first + t, 0, blocks - 1)
        partner = partners_ref[j, a]
        d = jnp.clip(partner - a, -REACH, REACH)
        ok = (partner >= 0) & (t < count)
        at = (((count - 3) * SLOTS + t) * (2 * REACH + 1) + d + REACH) * 2
        at = jnp.clip(at, 0, DIAG - 2)
        place_at[2 * i] = jnp.where(ok, consts_ref[at], ZERO)
        place_at[2 * i + 1] = jnp.where(ok, consts_ref[at + 1], ZERO)
        return 0

    def look_up():
        lax.fori_loop(OFFS[3], TOTAL, right_of, 0)
        partners_copy.wait()
        lax.fori_loop(0, SLOTS * partner_slots, place_of, 0)
        res[ZERO] = jnp.zeros(res.shape[1:], F32)

    step = min(256, half)

    def split(x):
        hi = x.astype(BF16)
        return hi, (x - hi.astype(F32)).astype(BF16)

    def prepare(load, at, left=True, right=True):
        def body(i, _):
            rows = pl.ds(pl.multiple_of(i * step, step), step)
            x = load(rows)
            if right:
                right_hi[at, rows, :], right_lo[at, rows, :] = split(x)
            if left:
                left_hi[at, :, rows], left_lo[at, :, rows] = split(x.T)
            return 0

        lax.fori_loop(0, depth // step, body, 0)

    def prepare_third(n):
        def body(i, _):
            rows = pl.ds(pl.multiple_of(n * half + i * step, step), step)
            lthird_hi[:, rows], lthird_lo[:, rows] = split(third[rows, :].T)
            return 0

        lax.fori_loop(0, half // step, body, 0)

    def times(lh, ll, rh, rl):
        total = jnp.dot(lh, rh, preferred_element_type=F32)
        total += jnp.dot(lh, rl, preferred_element_type=F32)
        return total + jnp.dot(ll, rh, preferred_element_type=F32)

    def store(total, g, i):
        for rank in range(RANKS):
            parts[g][rank % 2, rank // 2, i] = total[rank * SHARD : (rank + 1) * SHARD]

    def over(g, body, start=0, stop=None):
        def run(i, _):
            body(i)
            return 0

        lax.fori_loop(start, SIZES[g] if stop is None else stop, run, 0)

    def products(g, start=0, stop=None):
        def body(i):
            left = jnp.clip(consts_ref[NTAB + OFFS[g] + i], 0, B2)
            right = jnp.clip(consts_ref[NTAB + TOTAL + i + OFFS[g]], 0, B2) if g < 3 else right_at[OFFS[g] + i]
            store(times(left_hi[left], left_lo[left], right_hi[right], right_lo[right]), g, i)

        over(g, body, start, stop)

    def product_third():
        right = jnp.where(c == 0, count - 3, 2)
        total = times(lthird_hi[...], lthird_lo[...], right_hi[right], right_lo[right])
        for rank in range(RANKS):
            third_rows[rank] = total[rank * SHARD : (rank + 1) * SHARD]
        for copy in third_relays():
            copy.start()

    def third_relays():
        return (
            remote(third_rows.at[2 * across], third_relay.at[0], z1_send.at[LAST, 0], z1_recv.at[LAST, 0], dev_up),
            remote(
                third_rows.at[2 * across + 1], third_relay.at[1], z1_send.at[LAST, 1], z1_recv.at[LAST, 1], dev_down
            ),
        )

    def third_copies():
        copies = [
            remote(third_rows.at[2 * z + 1 - c], third_own, l_send.at[4], l_recv.at[4], dev_core),
        ]
        for core in range(2):
            to_up, to_down = (b, 2 * up + core), (b, 2 * down + core)
            copies.append(remote(third_up.at[core], third_sums.at[c], l_send.at[core], l_recv.at[c], to_up))
            copies.append(
                remote(third_down.at[core], third_sums.at[2 + c], l_send.at[2 + core], l_recv.at[2 + c], to_down)
            )
        return copies

    def relay_third():
        for copy in third_relays():
            copy.wait_recv()
        third_up[0] = third_rows[2 * up] + third_relay[0]
        third_up[1] = third_rows[2 * up + 1]
        third_down[0] = third_rows[2 * down]
        third_down[1] = third_rows[2 * down + 1] + third_relay[1]
        for copy in third_copies():
            copy.start()

    def sum_third():
        remote(third_rows.at[0], third_own, l_send.at[4], l_recv.at[4], dev_core).wait_recv()
        for source in range(4):
            remote(third_rows.at[0], third_sums.at[source], l_send.at[0], l_recv.at[source], dev_core).wait_recv()
        kept, other = third_rows[2 * z + c], third_own[...]
        for source in range(2):
            total = jnp.where(c == source, kept, other) + (third_sums[source] + third_sums[2 + source])
            res[OFFS[LAST] + source] = total
            rows_of[LAST][source] = total

    def core_copy(g):
        return remote(parts[g].at[1 - c], from_core[g], c_send.at[g], c_recv.at[g], dev_core)

    def relay_copies(g):
        upper, lower = out_across[g].at[:, pl.ds(0, 16)], out_across[g].at[:, pl.ds(16, 16)]
        return (
            remote(upper, relay_up[g], z1_send.at[g, 0], z1_recv.at[g, 0], dev_up),
            remote(lower, relay_down[g], z1_send.at[g, 1], z1_recv.at[g, 1], dev_down),
        )

    def sum_copies(g):
        return (
            remote(out_up[g], sum_up[g], z2_send.at[g, 0], z2_recv.at[g, 0], dev_up),
            remote(out_down[g], sum_down[g], z2_send.at[g, 1], z2_recv.at[g, 1], dev_down),
        )

    def add_core(g):
        core_copy(g).wait_recv()

        def add_across(i):
            out_across[g][i] = parts[g][c, across, i] + from_core[g][across, i]

        over(g, add_across)
        for copy in relay_copies(g):
            copy.start()

    def add_relay(g):
        for copy in relay_copies(g):
            copy.wait_recv()

        def add(i):
            total = parts[g][c, up, i] + from_core[g][up, i]
            out_up[g][i, :16, :] = total[:16] + relay_up[g][i]
            out_up[g][i, 16:, :] = total[16:]
            total = parts[g][c, down, i] + from_core[g][down, i]
            out_down[g][i, :16, :] = total[:16]
            out_down[g][i, 16:, :] = total[16:] + relay_down[g][i]

        over(g, add)
        for copy in sum_copies(g):
            copy.start()

    def forward_copies(g):
        copies = []
        if AHEAD[g]:
            src = rows_of[g].at[pl.ds(0, AHEAD[g])]
            copies.append(remote(src, from_before[g], f_send.at[g, 0], f_recv.at[g, 0], dev_after))
        if BEHIND[g]:
            src = rows_of[g].at[pl.ds(AHEAD[g], BEHIND[g])]
            copies.append(remote(src, from_after[g], f_send.at[g, 1], f_recv.at[g, 1], dev_before))
        return copies

    def forward(g):
        for copy in forward_copies(g):
            copy.start()

    def turn_copy(g, k):
        to = (r + k) % RANKS
        return remote(t_out[g].at[to], t_in[g].at[r], t_send.at[g, k], t_recv.at[g, k], (b, to))

    def turn_arrival(g, k):
        to, source = (r + k) % RANKS, (r + RANKS - k) % RANKS
        return remote(t_out[g].at[to], t_in[g].at[source], t_send.at[g, k], t_recv.at[g, k], (b, to))

    def finish(g):
        for copy in sum_copies(g):
            copy.wait_recv()

        def add(i):
            total = (parts[g][c, z, i] + from_core[g][z, i]) + (sum_up[g][i] + sum_down[g][i])
            res[OFFS[g] + i] = total
            rows_of[g][i] = total

        over(g, add)
        turn(g)

    def turn(g):
        turned = res[OFFS[g] : OFFS[g] + 4].reshape(4 * SHARD, RANKS * SHARD).T
        for rank in range(RANKS):
            t_out[g][rank] = turned[rank * SHARD : (rank + 1) * SHARD]

        def send(k, _):
            turn_copy(g, k).start()
            return 0

        lax.fori_loop(1, RANKS, send, 0)

    def collect(g):
        def arrive(k, _):
            turn_arrival(g, k).wait_recv()
            return 0

        lax.fori_loop(1, RANKS, arrive, 0)
        t_in[g][r] = t_out[g][r]
        pieces = [t_in[g][rank] for rank in range(RANKS)]
        for i in range(min(4, SIZES[g])):
            lanes = slice(SHARD * i, SHARD * (i + 1))
            res[RES_T + 4 * g + i] = jnp.concatenate([piece[:, lanes] for piece in pieces], axis=1)

    def prepare_own(t, _):
        prepare(lambda rows: own[t, rows, :], t)
        return 0

    def receive(g):
        for copy in forward_copies(g):
            copy.wait_recv()
        for i in range(AHEAD[g]):
            res[RES_FA[g] + i] = from_before[g][i]
        for i in range(BEHIND[g]):
            res[RES_FB[g] + i] = from_after[g][i]

    def place(start, stop):
        def body(i, _):
            block = res[place_at[2 * i]] + res[place_at[2 * i + 1]]
            pair_ref[i // partner_slots, i % partner_slots] = block * scale
            return 0

        lax.fori_loop(start * partner_slots, stop * partner_slots, body, 0)

    def place_diag():
        def body(t, _):
            at = jnp.where(t < count, jnp.clip(consts_ref[DIAG + t], 0, ZERO), ZERO)
            diag_ref[t] = res[at] * scale
            return 0

        lax.fori_loop(0, SLOTS, body, 0)

    lax.fori_loop(0, SLOTS, prepare_own, 0)

    def arrived(*numbers):
        for n in numbers:
            sends_a[n].wait_recv()
            sends_b[n].wait_recv()

    def prepare_in(k, **sides):
        prepare(lambda rows: inbox[k][rows, :], A1 + k, **sides)
        prepare(lambda rows: inbox[2 + k][rows, :], B1 + k, **sides)

    def multiply(g):
        products(g)
        core_copy(g).start()

    consts_copy.wait()
    multiply(0)
    multiply(1)
    add_core(0)
    multiply(2)
    add_core(1)
    add_relay(0)
    add_core(2)
    add_relay(1)
    look_up()
    finish(0)
    add_relay(2)

    arrived(0, 1)
    prepare_in(0)
    multiply(3)
    finish(1)
    multiply(4)
    collect(0)
    add_core(3)
    finish(2)
    add_core(4)
    add_relay(3)
    collect(1)
    add_relay(4)
    collect(2)
    finish(3)
    finish(4)
    collect(3)
    collect(4)

    arrived(2, 3)
    prepare_in(1, right=False)
    multiply(5)
    prepare_in(1, left=False)
    products(6, 0, 2)
    add_core(5)
    products(6, 2, 3)
    core_copy(6).start()
    add_core(6)
    add_relay(5)
    third_a[0].wait_recv()
    prepare_third(0)

    third_a[1].wait_recv()
    prepare_third(1)
    product_third()
    add_relay(6)
    for g in (3, 4):
        forward(g)
    relay_third()
    finish(5)
    forward(5)
    finish(6)
    forward(6)
    sum_third()
    forward(LAST)
    turn(LAST)
    collect(5)
    collect(6)
    for g in (3, 4, 5, 6):
        receive(g)
    place(3, SLOTS)
    place_diag()
    out_copies = [pltpu.make_async_copy(pair_ref.at[t], pair_hbm.at[t], out_sem.at[t]) for t in range(SLOTS)]
    out_copies.append(pltpu.make_async_copy(diag_ref, diag_hbm, out_sem.at[SLOTS]))
    for t in range(3, SLOTS + 1):
        out_copies[t].start()
    collect(LAST)
    receive(LAST)
    place(0, 3)
    for t in range(3):
        out_copies[t].start()

    for copy in out_copies:
        copy.wait()
    for n in range(len(chunks)):
        sends_a[n].wait_send()
        sends_b[n].wait_send()
    for copy in (*third_a, *third_relays()):
        copy.wait_send()
    for copy in third_copies():
        copy.wait_send()
    for g in range(GROUPS):
        copies = forward_copies(g)
        if g < LAST:
            copies += [core_copy(g), *relay_copies(g), *sum_copies(g)]
        for copy in copies:
            copy.wait_send()

        def sent(k, _, g=g):
            turn_copy(g, k).wait_send()
            return 0

        lax.fori_loop(1, RANKS, sent, 0)


def deliver(pair_in, diag_in, pair_ref, diag_ref, pair_held, diag_held, in_sem, out_sem):
    slots = pair_in.shape[0]
    steps = [(pair_in.at[t], pair_held.at[t], pair_ref.at[t]) for t in range(slots)]
    steps.append((diag_in, diag_held, diag_ref))
    loads = [pltpu.make_async_copy(src, held, in_sem.at[i]) for i, (src, held, _) in enumerate(steps)]
    stores = [pltpu.make_async_copy(held, dst, out_sem.at[i]) for i, (_, held, dst) in enumerate(steps)]
    for load in loads:
        load.start()
    for load, store in zip(loads, stores):
        load.wait()
        store.start()
    for store in stores:
        store.wait()


def local(blk_count, factors, partners, block_owner):
    slots, aux_dev, occ, nb = factors.shape
    depth = aux_dev * occ
    half = depth // 2
    groups = GROUPS
    dma = pltpu.SemaphoreType.DMA
    hbm = pl.BlockSpec(memory_space=pl.ANY)

    def room(*shape):
        return pltpu.VMEM((*shape, nb), F32)

    def by_group(*lead, rows=SHARD, sizes=SIZES):
        return [room(*lead, size, rows) for size in sizes]

    found = pl.pallas_call(
        functools.partial(kernel, blk_count),
        out_shape=[
            jax.ShapeDtypeStruct((slots, partners.shape[1], SHARD, nb), F32),
            jax.ShapeDtypeStruct((slots, SHARD, nb), F32),
        ],
        in_specs=[hbm] * 4,
        out_specs=[hbm, hbm],
        scratch_shapes=[
            pltpu.SMEM(block_owner.shape, I32),
            pltpu.SMEM(partners.shape[::-1], I32),
            pltpu.SMEM(CONSTS.shape, I32),
            room(slots, partners.shape[1], SHARD),
            room(slots, SHARD),
            room(3, half),
            room(slots, depth),
            [room(depth)] * 3,
            [room(depth)] * 4,
            pltpu.VMEM((9, nb, depth), BF16),
            pltpu.VMEM((9, nb, depth), BF16),
            pltpu.VMEM((9, depth, nb), BF16),
            pltpu.VMEM((9, depth, nb), BF16),
            pltpu.VMEM((nb, depth), BF16),
            pltpu.VMEM((nb, depth), BF16),
            by_group(2, ZDIM, sizes=SIZES[:LAST]),
            by_group(ZDIM, sizes=SIZES[:LAST]),
            by_group(sizes=SIZES[:LAST]),
            by_group(sizes=SIZES[:LAST]),
            by_group(sizes=SIZES[:LAST]),
            by_group(rows=SHARD // 2, sizes=SIZES[:LAST]),
            by_group(rows=SHARD // 2, sizes=SIZES[:LAST]),
            by_group(sizes=SIZES[:LAST]),
            by_group(sizes=SIZES[:LAST]),
            by_group(),
            by_group(sizes=[max(1, size) for size in AHEAD]),
            by_group(sizes=[max(1, size) for size in BEHIND]),
            room(depth),
            room(RANKS, SHARD),
            room(2, SHARD),
            room(2, SHARD),
            room(2, SHARD),
            room(4, SHARD),
            room(SHARD),
            [pltpu.VMEM((RANKS, SHARD, 4 * SHARD), F32)] * GROUPS,
            [pltpu.VMEM((RANKS, SHARD, 4 * SHARD), F32)] * GROUPS,
            room(NRES, SHARD),
            pltpu.SMEM((TOTAL,), I32),
            pltpu.SMEM((2 * slots * partners.shape[1],), I32),
            dma((3,)),
            dma((slots + 1,)),
            dma,
            dma((SLOTS,)),
            dma((2, 6)),
            dma((2, 6)),
            dma((groups,)),
            dma((groups,)),
            dma((groups, 2)),
            dma((groups, 2)),
            dma((groups, 2)),
            dma((groups, 2)),
            dma((groups, RANKS)),
            dma((groups, RANKS)),
            dma((groups, 2)),
            dma((groups, 2)),
            dma((5,)),
            dma((5,)),
        ],
        compiler_params=pltpu.CompilerParams(
            collective_id=0, has_side_effects=True, vmem_limit_bytes=60 * 1024 * 1024
        ),
    )(block_owner, partners.T, jnp.asarray(CONSTS), factors.reshape(slots, depth, nb))
    return pl.pallas_call(
        deliver,
        out_shape=[jax.ShapeDtypeStruct(array.shape, array.dtype) for array in found],
        in_specs=[hbm, hbm],
        out_specs=[hbm, hbm],
        scratch_shapes=[*(pltpu.VMEM(array.shape, F32) for array in found), dma((slots + 1,)), dma((slots + 1,))],
    )(*found)


def solution(mesh):
    in_specs = (P("blk", "aux", None, None), P(), P())
    out_specs = (P("blk", None, "aux", None), P("blk", "aux", None))
    return jax.shard_map(
        functools.partial(local, mesh.shape["blk"]),
        mesh=mesh,
        in_specs=in_specs,
        out_specs=out_specs,
        check_vma=False,
    )
```

```python
import functools
import math

import jax
import jax.numpy as jnp
import numpy as np
from jax import lax
from jax.experimental import pallas as pl
from jax.experimental.pallas import tpu as pltpu
from jax.sharding import PartitionSpec as P

MESH = pl.DeviceIdType.MESH
F32, BF16, I32 = jnp.float32, jnp.bfloat16, jnp.int32

SLOTS = 5
REACH = 5
RANKS = 8
ZDIM = 4
SHARD = 32

A1, A2, B1, B2, A3, B3 = 5, 6, 7, 8, 9, 10
FRONT, BACK = 16, 32


def _plan():
    own = [[(t, t + 1) for t in range(4)] + [(0, 0)]]
    own += [[(t, t + 2) for t in range(3)] + [(1, 1), (2, 2)]]
    own += [[(0, 3), (1, 4), (0, 4), (3, 3), (4, 4)]]
    first = [[(A1, BACK + s) for s in range(4)], [(B1, FRONT + t) for t in (1, 2, 3)]]
    second = [[(A2, BACK + 2), (A2, BACK + 3), (B2, FRONT + 2)]]
    second += [[(A1, BACK + 4), (B2, FRONT + 1), (B2, FRONT + 3), (B1, FRONT + 4)]]
    last = [[(A3, BACK + 2), (B3, FRONT + 2)]]
    return own + first + second + last


def _starts(sizes):
    return [sum(sizes[:g]) for g in range(len(sizes))]


PLAN = _plan()
GROUPS = len(PLAN)
LAST = GROUPS - 1
SIZES = [len(group) for group in PLAN]
OFFS = _starts(SIZES)
TOTAL = sum(SIZES)
AHEAD = [sum(key[0] in (A1, A2, A3) for key in group) for group in PLAN]
BEHIND = [sum(key[0] in (B1, B2, B3) for key in group) for group in PLAN]
RES_T = 36
RES_FA = [RES_T + 4 * GROUPS + start for start in _starts(AHEAD)]
RES_FB = [RES_FA[-1] + AHEAD[-1] + start for start in _starts(BEHIND)]
ZERO = RES_FB[-1] + BEHIND[-1]
NRES = ZERO + 1


def _tables():
    row, column, from_a, from_b = {}, {}, {}, {}
    for g, group in enumerate(PLAN):
        for i, key in enumerate(group):
            row[key] = OFFS[g] + i
            if i < 4:
                column[key] = RES_T + 4 * g + i
            if key[0] in (A1, A2, A3):
                from_a[key] = RES_FA[g] + i
            elif key[0] in (B1, B2, B3):
                from_b[key] = RES_FB[g] + i - AHEAD[g]
    table = np.full((3, SLOTS, 2 * REACH + 1, 2), ZERO, np.int32)
    aheads, behinds = (A1, A2, A3), (B1, B2, B3)
    for n in (3, 4, 5):
        for t in range(n):
            for d in range(1, REACH + 1):
                p = t + d
                if p < n:
                    places = [row[(t, p)]]
                else:
                    k, s = p - n + 1, n - 1 - t
                    places = []
                    if k <= 3 and (aheads[k - 1], BACK + s) in column:
                        places.append(column[(aheads[k - 1], BACK + s)])
                    if s <= 2 and (behinds[s], FRONT + k - 1) in from_b:
                        places.append(from_b[(behinds[s], FRONT + k - 1)])
                assert len(places) == (2 if p >= n and (k, s) == (3, 2) else 1), (n, t, d)
                table[n - 3, t, REACH + d, : len(places)] = places
                q = t - d
                if q >= 0:
                    places = [column[(q, t)]]
                else:
                    k = -q
                    places = []
                    if k <= 3 and (behinds[k - 1], FRONT + t) in column:
                        places.append(column[(behinds[k - 1], FRONT + t)])
                    if t <= 2 and (aheads[t], BACK + k - 1) in from_a:
                        places.append(from_a[(aheads[t], BACK + k - 1)])
                assert len(places) == (2 if q < 0 and (k, t) == (3, 2) else 1), (n, t, -d)
                table[n - 3, t, REACH - d, : len(places)] = places
    return np.concatenate([table.reshape(-1), [row[(t, t)] for t in range(SLOTS)]]).astype(np.int32)


TABLE = _tables()
NTAB = TABLE.shape[0]
DIAG = NTAB - SLOTS
LEFT = np.array([key[0] for group in PLAN for key in group], np.int32)
RIGHT = np.array([key[1] for group in PLAN for key in group], np.int32)
CONSTS = np.concatenate([TABLE, LEFT, RIGHT])


def kernel(
    blk_count,
    owner_hbm,
    partners_hbm,
    consts_hbm,
    fac_ref,
    pair_hbm,
    diag_hbm,
    owner_ref,
    partners_ref,
    consts_ref,
    pair_ref,
    diag_ref,
    head,
    own,
    staged,
    inbox,
    left_hi,
    left_lo,
    right_hi,
    right_lo,
    lthird_hi,
    lthird_lo,
    parts,
    from_core,
    out_across,
    out_up,
    out_down,
    relay_up,
    relay_down,
    sum_up,
    sum_down,
    rows_of,
    from_before,
    from_after,
    third,
    third_rows,
    third_up,
    third_down,
    third_relay,
    third_sums,
    third_own,
    t_out,
    t_in,
    res,
    right_at,
    place_at,
    scalar_sem,
    out_sem,
    head_sem,
    own_sem,
    y_send,
    y_recv,
    c_send,
    c_recv,
    z1_send,
    z1_recv,
    z2_send,
    z2_recv,
    t_send,
    t_recv,
    f_send,
    f_recv,
    l_send,
    l_recv,
):
    depth = own.shape[1]
    half = depth // 2
    blocks = owner_ref.shape[0]
    partner_slots = partners_ref.shape[0]
    scale = 1.0 / math.sqrt(RANKS * depth)

    b, r = lax.axis_index("blk"), lax.axis_index("aux")
    z, c = r // 2, r % 2
    after, before = (b + 1) % blk_count, (b + blk_count - 1) % blk_count
    up, down, across = (z + 1) % ZDIM, (z + 3) % ZDIM, (z + 2) % ZDIM
    dev_after, dev_before = (after, r), (before, r)
    dev_core = (b, 2 * z + 1 - c)
    dev_up, dev_down = (b, 2 * up + c), (b, 2 * down + c)

    owner_copy = pltpu.make_async_copy(owner_hbm, owner_ref, scalar_sem.at[0])
    owner_copy.start()
    partners_copy = pltpu.make_async_copy(partners_hbm, partners_ref, scalar_sem.at[1])
    consts_copy = pltpu.make_async_copy(consts_hbm, consts_ref, scalar_sem.at[2])
    head_copy = pltpu.make_async_copy(fac_ref.at[pl.ds(2, 3), pl.ds(0, half)], head, head_sem)
    head_copy.start()
    own_copies = [pltpu.make_async_copy(fac_ref.at[t], own.at[t], own_sem.at[t]) for t in range(SLOTS)]
    for t in (4, 3, 2, 1, 0):
        own_copies[t].start()

    barrier = pltpu.get_barrier_semaphore()
    peers = [(b, (r + k) % RANKS) for k in range(1, RANKS)] + [dev_after, dev_before]
    for peer in peers:
        pl.semaphore_signal(barrier, inc=1, device_id=peer, device_id_type=MESH)

    partners_copy.start()
    consts_copy.start()
    owner_copy.wait()

    def tally(i, carry):
        count, first = carry
        holder = owner_ref[i]
        return count + (holder == b).astype(I32), first + (holder < b).astype(I32)

    count, first = lax.fori_loop(0, blocks, tally, (jnp.int32(0), jnp.int32(0)))
    count = jnp.clip(count, 3, SLOTS)

    head_copy.wait()

    def stage_head(i, _):
        rows = pl.ds(pl.multiple_of(i * 64, 64), 64)
        staged[0][rows, :] = head[count - 3, rows, :]
        return 0

    lax.fori_loop(0, half // 64, stage_head, 0)
    pl.semaphore_wait(barrier, len(peers))

    def remote(src, dst, send, recv, device):
        return pltpu.make_async_remote_copy(
            src_ref=src, dst_ref=dst, send_sem=send, recv_sem=recv, device_id=device, device_id_type=MESH
        )

    chunks = [(k, half * i) for k in range(2) for i in range(2)]
    sends_a, sends_b = [], []
    for n, (k, start) in enumerate(chunks):
        rows = pl.ds(start, half)
        sends_a.append(remote(fac_ref.at[k, rows], inbox[k].at[rows], y_send.at[0, n], y_recv.at[0, n], dev_before))
        sends_b.append(
            remote(staged[k].at[rows], inbox[2 + k].at[rows], y_send.at[1, n], y_recv.at[1, n], dev_after)
        )

    third_a, third_b = [], []
    for n in range(2):
        rows, sems = pl.ds(half * n, half), (y_send.at[0, 4 + n], y_recv.at[0, 4 + n])
        third_a.append(remote(fac_ref.at[2, rows], third.at[rows], *sems, dev_before))
        third_b.append(remote(staged[2].at[rows], third.at[rows], *sems, dev_after))

    sends_a[0].start()
    sends_b[0].start()
    for n in range(1, len(chunks)):
        sends_a[n].start()

    @pl.when(c == 0)
    def _():
        for copy in third_a:
            copy.start()

    for t in (4, 3, 2, 1, 0):
        own_copies[t].wait()

    def stage(k, start):
        def move(i, _):
            rows = pl.ds(pl.multiple_of(start + i * 64, 64), 64)
            staged[k][rows, :] = own[count - 1 - k, rows, :]
            return 0

        lax.fori_loop(0, half // 64, move, 0)

    for n in range(1, len(chunks)):
        stage(*chunks[n])
        sends_b[n].start()

    @pl.when(c == 1)
    def _():
        for n in range(2):
            stage(2, half * n)
            third_b[n].start()

    def right_of(e, _):
        code = consts_ref[NTAB + TOTAL + e]
        s, t = code - BACK, code - FRONT
        from_back = jnp.where(s < count, count - 1 - s, B1 + s - count)
        from_front = jnp.where(t < count, t, A1 + t - count)
        right = jnp.where(code >= BACK, from_back, jnp.where(code >= FRONT, from_front, code))
        right_at[e] = jnp.clip(right, 0, B2)
        return 0


    def place_of(i, _):
        t, j = i // partner_slots, i % partner_slots
        a = jnp.clip(first + t, 0, blocks - 1)
        partner = partners_ref[j, a]
        d = jnp.clip(partner - a, -REACH, REACH)
        ok = (partner >= 0) & (t < count)
        at = (((count - 3) * SLOTS + t) * (2 * REACH + 1) + d + REACH) * 2
        at = jnp.clip(at, 0, DIAG - 2)
        place_at[2 * i] = jnp.where(ok, consts_ref[at], ZERO)
        place_at[2 * i + 1] = jnp.where(ok, consts_ref[at + 1], ZERO)
        return 0

    def look_up():
        lax.fori_loop(OFFS[3], TOTAL, right_of, 0)
        partners_copy.wait()
        lax.fori_loop(0, SLOTS * partner_slots, place_of, 0)
        res[ZERO] = jnp.zeros(res.shape[1:], F32)

    step = min(256, half)

    def split(x):
        hi = x.astype(BF16)
        return hi, (x - hi.astype(F32)).astype(BF16)

    def prepare(load, at, left=True, right=True, start=0, stop=depth):
        def body(i, _):
            rows = pl.ds(pl.multiple_of(i * step, step), step)
            x = load(rows)
            if right:
                right_hi[at, rows, :], right_lo[at, rows, :] = split(x)
            if left:
                left_hi[at, :, rows], left_lo[at, :, rows] = split(x.T)
            return 0

        lax.fori_loop(start // step, stop // step, body, 0)

    def prepare_third(n):
        def body(i, _):
            rows = pl.ds(pl.multiple_of(n * half + i * step, step), step)
            lthird_hi[:, rows], lthird_lo[:, rows] = split(third[rows, :].T)
            return 0

        lax.fori_loop(0, half // step, body, 0)

    def times(lh, ll, rh, rl):
        total = jnp.dot(lh, rh, preferred_element_type=F32)
        total += jnp.dot(lh, rl, preferred_element_type=F32)
        return total + jnp.dot(ll, rh, preferred_element_type=F32)

    def store(total, g, i):
        for rank in range(RANKS):
            parts[g][rank % 2, rank // 2, i] = total[rank * SHARD : (rank + 1) * SHARD]

    def over(g, body, start=0, stop=None):
        def run(i, _):
            body(i)
            return 0

        lax.fori_loop(start, SIZES[g] if stop is None else stop, run, 0)

    def products(g, start=0, stop=None):
        def body(i):
            left = jnp.clip(consts_ref[NTAB + OFFS[g] + i], 0, B2)
            right = jnp.clip(consts_ref[NTAB + TOTAL + i + OFFS[g]], 0, B2) if g < 3 else right_at[OFFS[g] + i]
            store(times(left_hi[left], left_lo[left], right_hi[right], right_lo[right]), g, i)

        over(g, body, start, stop)

    def product_third():
        right = jnp.where(c == 0, count - 3, 2)
        total = times(lthird_hi[...], lthird_lo[...], right_hi[right], right_lo[right])
        for rank in range(RANKS):
            third_rows[rank] = total[rank * SHARD : (rank + 1) * SHARD]
        for copy in third_relays():
            copy.start()

    def third_relays():
        return (
            remote(third_rows.at[2 * across], third_relay.at[0], z1_send.at[LAST, 0], z1_recv.at[LAST, 0], dev_up),
            remote(
                third_rows.at[2 * across + 1], third_relay.at[1], z1_send.at[LAST, 1], z1_recv.at[LAST, 1], dev_down
            ),
        )

    def third_copies():
        copies = [
            remote(third_rows.at[2 * z + 1 - c], third_own, l_send.at[4], l_recv.at[4], dev_core),
        ]
        for core in range(2):
            to_up, to_down = (b, 2 * up + core), (b, 2 * down + core)
            copies.append(remote(third_up.at[core], third_sums.at[c], l_send.at[core], l_recv.at[c], to_up))
            copies.append(
                remote(third_down.at[core], third_sums.at[2 + c], l_send.at[2 + core], l_recv.at[2 + c], to_down)
            )
        return copies

    def relay_third():
        for copy in third_relays():
            copy.wait_recv()
        third_up[0] = third_rows[2 * up] + third_relay[0]
        third_up[1] = third_rows[2 * up + 1]
        third_down[0] = third_rows[2 * down]
        third_down[1] = third_rows[2 * down + 1] + third_relay[1]
        for copy in third_copies():
            copy.start()

    def sum_third():
        remote(third_rows.at[0], third_own, l_send.at[4], l_recv.at[4], dev_core).wait_recv()
        for source in range(4):
            remote(third_rows.at[0], third_sums.at[source], l_send.at[0], l_recv.at[source], dev_core).wait_recv()
        kept, other = third_rows[2 * z + c], third_own[...]
        for source in range(2):
            total = jnp.where(c == source, kept, other) + (third_sums[source] + third_sums[2 + source])
            res[OFFS[LAST] + source] = total
            rows_of[LAST][source] = total

    def core_copy(g):
        return remote(parts[g].at[1 - c], from_core[g], c_send.at[g], c_recv.at[g], dev_core)

    def relay_copies(g):
        upper, lower = out_across[g].at[:, pl.ds(0, 16)], out_across[g].at[:, pl.ds(16, 16)]
        return (
            remote(upper, relay_up[g], z1_send.at[g, 0], z1_recv.at[g, 0], dev_up),
            remote(lower, relay_down[g], z1_send.at[g, 1], z1_recv.at[g, 1], dev_down),
        )

    def sum_copies(g):
        return (
            remote(out_up[g], sum_up[g], z2_send.at[g, 0], z2_recv.at[g, 0], dev_up),
            remote(out_down[g], sum_down[g], z2_send.at[g, 1], z2_recv.at[g, 1], dev_down),
        )

    def add_core(g):
        core_copy(g).wait_recv()

        def add_across(i):
            out_across[g][i] = parts[g][c, across, i] + from_core[g][across, i]

        over(g, add_across)
        for copy in relay_copies(g):
            copy.start()

    def add_relay(g):
        for copy in relay_copies(g):
            copy.wait_recv()

        def add(i):
            total = parts[g][c, up, i] + from_core[g][up, i]
            out_up[g][i, :16, :] = total[:16] + relay_up[g][i]
            out_up[g][i, 16:, :] = total[16:]
            total = parts[g][c, down, i] + from_core[g][down, i]
            out_down[g][i, :16, :] = total[:16]
            out_down[g][i, 16:, :] = total[16:] + relay_down[g][i]

        over(g, add)
        for copy in sum_copies(g):
            copy.start()

    def forward_copies(g):
        copies = []
        if AHEAD[g]:
            src = rows_of[g].at[pl.ds(0, AHEAD[g])]
            copies.append(remote(src, from_before[g], f_send.at[g, 0], f_recv.at[g, 0], dev_after))
        if BEHIND[g]:
            src = rows_of[g].at[pl.ds(AHEAD[g], BEHIND[g])]
            copies.append(remote(src, from_after[g], f_send.at[g, 1], f_recv.at[g, 1], dev_before))
        return copies

    def forward(g):
        for copy in forward_copies(g):
            copy.start()

    def turn_copy(g, k):
        to = (r + k) % RANKS
        return remote(t_out[g].at[to], t_in[g].at[r], t_send.at[g, k], t_recv.at[g, k], (b, to))

    def turn_arrival(g, k):
        to, source = (r + k) % RANKS, (r + RANKS - k) % RANKS
        return remote(t_out[g].at[to], t_in[g].at[source], t_send.at[g, k], t_recv.at[g, k], (b, to))

    def finish(g):
        for copy in sum_copies(g):
            copy.wait_recv()

        def add(i):
            total = (parts[g][c, z, i] + from_core[g][z, i]) + (sum_up[g][i] + sum_down[g][i])
            res[OFFS[g] + i] = total
            rows_of[g][i] = total

        over(g, add)
        turn(g)

    def turn(g):
        turned = res[OFFS[g] : OFFS[g] + 4].reshape(4 * SHARD, RANKS * SHARD).T
        for rank in range(RANKS):
            t_out[g][rank] = turned[rank * SHARD : (rank + 1) * SHARD]

        def send(k, _):
            turn_copy(g, k).start()
            return 0

        lax.fori_loop(1, RANKS, send, 0)

    def collect(g):
        def arrive(k, _):
            turn_arrival(g, k).wait_recv()
            return 0

        lax.fori_loop(1, RANKS, arrive, 0)
        t_in[g][r] = t_out[g][r]
        pieces = [t_in[g][rank] for rank in range(RANKS)]
        for i in range(min(4, SIZES[g])):
            lanes = slice(SHARD * i, SHARD * (i + 1))
            res[RES_T + 4 * g + i] = jnp.concatenate([piece[:, lanes] for piece in pieces], axis=1)

    def prepare_own(t, _):
        prepare(lambda rows: own[t, rows, :], t)
        return 0

    def receive(g):
        for copy in forward_copies(g):
            copy.wait_recv()
        for i in range(AHEAD[g]):
            res[RES_FA[g] + i] = from_before[g][i]
        for i in range(BEHIND[g]):
            res[RES_FB[g] + i] = from_after[g][i]

    def place(start, stop):
        def body(i, _):
            block = res[place_at[2 * i]] + res[place_at[2 * i + 1]]
            pair_ref[i // partner_slots, i % partner_slots] = block * scale
            return 0

        lax.fori_loop(start * partner_slots, stop * partner_slots, body, 0)

    def place_diag():
        def body(t, _):
            at = jnp.where(t < count, jnp.clip(consts_ref[DIAG + t], 0, ZERO), ZERO)
            diag_ref[t] = res[at] * scale
            return 0

        lax.fori_loop(0, SLOTS, body, 0)

    lax.fori_loop(0, SLOTS, prepare_own, 0)

    def arrived(*numbers):
        for n in numbers:
            sends_a[n].wait_recv()
            sends_b[n].wait_recv()

    def prepare_in(k, **sides):
        prepare(lambda rows: inbox[k][rows, :], A1 + k, **sides)
        prepare(lambda rows: inbox[2 + k][rows, :], B1 + k, **sides)

    def multiply(g):
        products(g)
        core_copy(g).start()

    consts_copy.wait()
    multiply(0)
    multiply(1)
    add_core(0)
    multiply(2)
    add_core(1)
    add_relay(0)
    add_core(2)
    add_relay(1)
    look_up()
    finish(0)
    add_relay(2)

    arrived(0, 1)
    prepare_in(0)
    multiply(3)
    finish(1)
    multiply(4)
    collect(0)
    add_core(3)
    finish(2)
    add_core(4)
    add_relay(3)
    collect(1)
    add_relay(4)
    collect(2)
    finish(3)
    finish(4)
    collect(3)
    collect(4)

    arrived(2)
    prepare_in(1, right=False, stop=half)
    arrived(3)
    prepare_in(1, right=False, start=half)
    multiply(5)
    prepare_in(1, left=False)
    products(6, 0, 2)
    add_core(5)
    products(6, 2, 4)
    core_copy(6).start()
    add_core(6)
    add_relay(5)
    third_a[0].wait_recv()
    prepare_third(0)

    third_a[1].wait_recv()
    prepare_third(1)
    product_third()
    add_relay(6)
    for g in (3, 4):
        forward(g)
    relay_third()
    finish(5)
    forward(5)
    finish(6)
    forward(6)
    sum_third()
    forward(LAST)
    turn(LAST)
    collect(5)
    collect(6)
    for g in (3, 4, 5, 6):
        receive(g)
    place(3, SLOTS)
    place_diag()
    out_copies = [pltpu.make_async_copy(pair_ref.at[t], pair_hbm.at[t], out_sem.at[t]) for t in range(SLOTS)]
    out_copies.append(pltpu.make_async_copy(diag_ref, diag_hbm, out_sem.at[SLOTS]))
    for t in range(3, SLOTS + 1):
        out_copies[t].start()
    collect(LAST)
    receive(LAST)
    place(0, 3)
    for t in range(3):
        out_copies[t].start()

    for copy in out_copies:
        copy.wait()
    for n in range(len(chunks)):
        sends_a[n].wait_send()
        sends_b[n].wait_send()
    for copy in (*third_a, *third_relays()):
        copy.wait_send()
    for copy in third_copies():
        copy.wait_send()
    for g in range(GROUPS):
        copies = forward_copies(g)
        if g < LAST:
            copies += [core_copy(g), *relay_copies(g), *sum_copies(g)]
        for copy in copies:
            copy.wait_send()

        def sent(k, _, g=g):
            turn_copy(g, k).wait_send()
            return 0

        lax.fori_loop(1, RANKS, sent, 0)


def deliver(pair_in, diag_in, pair_ref, diag_ref, pair_held, diag_held, in_sem, out_sem):
    slots = pair_in.shape[0]
    steps = [(pair_in.at[t], pair_held.at[t], pair_ref.at[t]) for t in range(slots)]
    steps.append((diag_in, diag_held, diag_ref))
    loads = [pltpu.make_async_copy(src, held, in_sem.at[i]) for i, (src, held, _) in enumerate(steps)]
    stores = [pltpu.make_async_copy(held, dst, out_sem.at[i]) for i, (_, held, dst) in enumerate(steps)]
    for load in loads:
        load.start()
    for load, store in zip(loads, stores):
        load.wait()
        store.start()
    for store in stores:
        store.wait()


def local(blk_count, factors, partners, block_owner):
    slots, aux_dev, occ, nb = factors.shape
    depth = aux_dev * occ
    half = depth // 2
    groups = GROUPS
    dma = pltpu.SemaphoreType.DMA
    hbm = pl.BlockSpec(memory_space=pl.ANY)

    def room(*shape):
        return pltpu.VMEM((*shape, nb), F32)

    def by_group(*lead, rows=SHARD, sizes=SIZES):
        return [room(*lead, size, rows) for size in sizes]

    found = pl.pallas_call(
        functools.partial(kernel, blk_count),
        out_shape=[
            jax.ShapeDtypeStruct((slots, partners.shape[1], SHARD, nb), F32),
            jax.ShapeDtypeStruct((slots, SHARD, nb), F32),
        ],
        in_specs=[hbm] * 4,
        out_specs=[hbm, hbm],
        scratch_shapes=[
            pltpu.SMEM(block_owner.shape, I32),
            pltpu.SMEM(partners.shape[::-1], I32),
            pltpu.SMEM(CONSTS.shape, I32),
            room(slots, partners.shape[1], SHARD),
            room(slots, SHARD),
            room(3, half),
            room(slots, depth),
            [room(depth)] * 3,
            [room(depth)] * 4,
            pltpu.VMEM((9, nb, depth), BF16),
            pltpu.VMEM((9, nb, depth), BF16),
            pltpu.VMEM((9, depth, nb), BF16),
            pltpu.VMEM((9, depth, nb), BF16),
            pltpu.VMEM((nb, depth), BF16),
            pltpu.VMEM((nb, depth), BF16),
            by_group(2, ZDIM, sizes=SIZES[:LAST]),
            by_group(ZDIM, sizes=SIZES[:LAST]),
            by_group(sizes=SIZES[:LAST]),
            by_group(sizes=SIZES[:LAST]),
            by_group(sizes=SIZES[:LAST]),
            by_group(rows=SHARD // 2, sizes=SIZES[:LAST]),
            by_group(rows=SHARD // 2, sizes=SIZES[:LAST]),
            by_group(sizes=SIZES[:LAST]),
            by_group(sizes=SIZES[:LAST]),
            by_group(),
            by_group(sizes=[max(1, size) for size in AHEAD]),
            by_group(sizes=[max(1, size) for size in BEHIND]),
            room(depth),
            room(RANKS, SHARD),
            room(2, SHARD),
            room(2, SHARD),
            room(2, SHARD),
            room(4, SHARD),
            room(SHARD),
            [pltpu.VMEM((RANKS, SHARD, 4 * SHARD), F32)] * GROUPS,
            [pltpu.VMEM((RANKS, SHARD, 4 * SHARD), F32)] * GROUPS,
            room(NRES, SHARD),
            pltpu.SMEM((TOTAL,), I32),
            pltpu.SMEM((2 * slots * partners.shape[1],), I32),
            dma((3,)),
            dma((slots + 1,)),
            dma,
            dma((SLOTS,)),
            dma((2, 6)),
            dma((2, 6)),
            dma((groups,)),
            dma((groups,)),
            dma((groups, 2)),
            dma((groups, 2)),
            dma((groups, 2)),
            dma((groups, 2)),
            dma((groups, RANKS)),
            dma((groups, RANKS)),
            dma((groups, 2)),
            dma((groups, 2)),
            dma((5,)),
            dma((5,)),
        ],
        compiler_params=pltpu.CompilerParams(
            collective_id=0, has_side_effects=True, vmem_limit_bytes=60 * 1024 * 1024
        ),
    )(block_owner, partners.T, jnp.asarray(CONSTS), factors.reshape(slots, depth, nb))
    return pl.pallas_call(
        deliver,
        out_shape=[jax.ShapeDtypeStruct(array.shape, array.dtype) for array in found],
        in_specs=[hbm, hbm],
        out_specs=[hbm, hbm],
        scratch_shapes=[*(pltpu.VMEM(array.shape, F32) for array in found), dma((slots + 1,)), dma((slots + 1,))],
    )(*found)


def solution(mesh):
    in_specs = (P("blk", "aux", None, None), P(), P())
    out_specs = (P("blk", None, "aux", None), P("blk", "aux", None))
    return jax.shard_map(
        functools.partial(local, mesh.shape["blk"]),
        mesh=mesh,
        in_specs=in_specs,
        out_specs=out_specs,
        check_vma=False,
    )
```
